128 devices in a mesh: ctx: 8 (over x, core), head: 16 (over z, y).
Axes of the slice: x: 4, y: 4, z: 4, core: 2. Of those that a mesh axis runs over, the one named last changes fastest.
Arguments:
- inputs: bfloat16 [512, 16384], P('head', 'ctx'), may hold values from -6 to 6
- gate: bfloat16 [512, 16384], P('head', 'ctx'), may hold values from -6 to 6
- filter_taps: float32 [512, 16384], P('head', 'ctx'), may hold values from -0.078125 to 0.078125
- skip: float32 [512], P('head'), may hold values from 0.5 to 1.5
- w_out: bfloat16 [512, 512], P('head'), may hold values from -0.25 to 0.25
- far_pairs: int32 [16, 4], P('ctx'), may hold values from -1 to 13, as said below
Outputs:
- projected: float32 [512, 16384], P('head', 'ctx')
The draws below stay inside these ranges and needn't reach their ends.
Inputs may be any that keep to these rules, and one draw needn't show every extreme that they name: `far_pairs`: row i lists i - 2 first when i >= 2, else -1; its other entries are distinct blocks below i - 2, or -1 where fewer exist.
All inputs are finite; a program needn't handle non-finite values.
Results may differ from the reference program's by a relative error of at most 0.0029.
Values may be sent and summed in bfloat16 or wider, within the bound.
A program may use at most 128 MiB of HBM per device.

```python
import jax
import jax.numpy as jnp

CHANNELS = 512
BLOCK = 1024
BLOCKS = 16
TOKENS = 16384
WIN = 2
FAR_SEL = 4


def draw_far_pairs(key, part):
    out_rows = jnp.arange(BLOCKS, dtype=jnp.int32)[:, None]
    in_cols = jnp.arange(BLOCKS, dtype=jnp.int32)[None, :]
    scores = jax.random.randint(key, (BLOCKS, BLOCKS), 0, 1 << 20, dtype=jnp.int32) * BLOCKS + in_cols
    usable = in_cols <= out_rows - WIN - 1
    scores = jnp.where(usable, scores, (1 << 30) + in_cols)
    ordering = jnp.argsort(scores, axis=1, stable=True)[:, :FAR_SEL - 1].astype(jnp.int32)
    picked_ok = jnp.take_along_axis(usable, ordering, axis=1)
    others = jnp.where(picked_ok, ordering, -1)
    leading = jnp.where(out_rows >= WIN, out_rows - WIN, -1)
    return jnp.concatenate([leading, others], axis=1).astype(jnp.int32)


def steps_of(key, dims, cuts, low, top_value):
    gain, own = 1.0, jax.random.fold_in(key, 6)
    for dim, shards_of in cuts:
        heights = jnp.exp(jax.random.uniform(jax.random.fold_in(own, dim), (shards_of,), jnp.float32, low / len(cuts), top_value / len(cuts)))
        gain = gain * jnp.repeat(heights, dims[dim] // shards_of).reshape([-1 if axis == dim else 1 for axis in range(len(dims))])
    return gain


def gaussian(key, dims, scale, limit, shards=(), held_as=jnp.bfloat16):
    drawn = jax.random.normal(key, dims, jnp.float32) * scale
    if len(shards) > 0:
        drawn = steps_of(key, dims, shards, -0.22, 0.18) * drawn
    return jnp.clip(drawn, min=-limit, max=limit).astype(held_as)


def setup_inputs(seed: int = 0) -> dict:
    streams_of = jax.random.split(jax.random.key(seed), 7)
    inputs = gaussian(streams_of[0], (CHANNELS, TOKENS), 1.0, 6.0, ((0, 16), (1, 8)))
    gate = gaussian(streams_of[1], (CHANNELS, TOKENS), 1.0, 6.0, ((0, 16), (1, 8)))
    filter_taps = gaussian(streams_of[2], (CHANNELS, TOKENS), (BLOCK * (WIN + FAR_SEL)) ** -0.5, 0.078125, ((0, 16), (1, 8)), jnp.float32)
    skip = jnp.clip(0.5 + 1.0 * jax.random.uniform(streams_of[3], (CHANNELS,), jnp.float32) ** steps_of(streams_of[3], (CHANNELS,), ((0, 16),), -0.2, 0.2), 0.5, 1.5)
    w_out = gaussian(streams_of[4], (CHANNELS, CHANNELS), CHANNELS ** -0.5, 0.25, ((0, 16),))
    far_pairs = draw_far_pairs(jax.random.fold_in(streams_of[6], 71), 0)
    return dict(inputs=inputs, gate=gate, filter_taps=filter_taps, skip=skip, w_out=w_out, far_pairs=far_pairs)


def reference(inputs, gate, filter_taps, skip, w_out, far_pairs):
    channels = inputs.shape[0]
    signal = inputs.astype(jnp.float32).reshape(channels, BLOCKS, BLOCK)
    padded = jnp.concatenate([signal, jnp.zeros_like(signal)], axis=-1)
    input_spec = jnp.fft.rfft(padded, axis=-1)
    tap_blocks = filter_taps.reshape(channels, BLOCKS, BLOCK)
    previous = jnp.concatenate([jnp.zeros_like(tap_blocks[:, :1]), tap_blocks[:, :-1]], axis=1)
    segments = jnp.concatenate([tap_blocks, previous], axis=-1)
    lag_spec = jnp.fft.rfft(segments, axis=-1)
    out_rows = jnp.arange(BLOCKS, dtype=jnp.int32)[:, None]
    in_cols = jnp.arange(BLOCKS, dtype=jnp.int32)[None, :]
    offsets = out_rows - in_cols
    near_ok = (offsets >= 0) & (offsets < WIN)
    far_ok = jnp.any(far_pairs[:, :, None] == in_cols[:, None, :], axis=1)
    weight = (near_ok | far_ok).astype(jnp.float32)
    pieces = []
    for target in range(BLOCKS):
        lag_index = jnp.clip(target - jnp.arange(BLOCKS, dtype=jnp.int32), 0, BLOCKS - 1)
        chosen = lag_spec[:, lag_index, :]
        summed = jnp.sum(chosen * input_spec * weight[target][None, :, None], axis=1)
        pieces.append(jnp.fft.irfft(summed, n=2 * BLOCK, axis=-1)[:, :BLOCK])
    conv = jnp.concatenate(pieces, axis=-1)
    mixed = (gate.astype(jnp.float32) * (conv + skip[:, None] * inputs.astype(jnp.float32))).astype(jnp.bfloat16)
    return jnp.dot(w_out.T, mixed, preferred_element_type=jnp.float32)
```

```python
import jax
import jax.numpy as jnp
from jax import lax
from jax.experimental import pallas as pl
from jax.experimental.pallas import tpu as pltpu
from jax.sharding import PartitionSpec as P

F32 = jnp.float32
BF16 = jnp.bfloat16
LANES = 128
BLOCKS = 16
SUBS = 8
PIECES = BLOCKS * SUBS
NC = 8
NH = 16
CH = 32
MINE = CH // NC
ROWS = 16
PER = 3 * ROWS
WIN = 2
MESH = pl.DeviceIdType.MESH


def greet(me_c, me_h):
    barrier = pltpu.get_barrier_semaphore()
    for k in range(1, NC):
        pl.semaphore_signal(
            barrier, inc=1, device_id={"ctx": lax.rem(me_c + k, NC)}, device_id_type=MESH
        )
    for k in range(1, NH):
        pl.semaphore_signal(
            barrier, inc=1, device_id={"head": lax.rem(me_h + k, NH)}, device_id_type=MESH
        )
    pl.semaphore_wait(barrier, NC - 1 + NH - 1)


def spread_kernel(
    x_ref, g_ref, h_ref, w_ref, far_ref, got, far_got, w_got,
    stage, packed, far_mine, send_sem, recv_sem, far_send, far_recv, w_send, w_recv, own_sem,
):
    me_c, me_h = lax.axis_index("ctx"), lax.axis_index("head")
    row = lax.broadcasted_iota(jnp.int32, (8, LANES), 0)
    table = jnp.full((8, LANES), -1, jnp.int32)
    for r in range(2):
        for k in range(4):
            table = jnp.where(row == 4 * r + k, far_ref[r, k], table)
    far_mine[...] = table
    greet(me_c, me_h)

    def w_copy(k):
        peer = lax.rem(me_h + k, NH)
        return pltpu.make_async_remote_copy(
            src_ref=w_ref, dst_ref=w_got.at[me_h], send_sem=w_send.at[k], recv_sem=w_recv.at[k],
            device_id={"head": peer}, device_id_type=MESH,
        )

    def far_copy(k):
        peer = lax.rem(me_c + k, NC)
        return pltpu.make_async_remote_copy(
            src_ref=far_mine, dst_ref=far_got.at[me_c], send_sem=far_send.at[k], recv_sem=far_recv.at[k],
            device_id={"ctx": peer}, device_id_type=MESH,
        )

    def copy(k):
        peer = lax.rem(me_c + k, NC)
        return pltpu.make_async_remote_copy(
            src_ref=packed.at[peer], dst_ref=got.at[me_c], send_sem=send_sem.at[k], recv_sem=recv_sem.at[k],
            device_id={"ctx": peer}, device_id_type=MESH,
        )

    for k in range(1, NC):
        far_copy(k).start()
    for a, ref in enumerate((h_ref, x_ref, g_ref)):
        for s in range(ROWS):
            stage[a, pl.ds(s, CH, stride=ROWS), :] = ref[:, LANES * s : LANES * (s + 1)].astype(F32)
        for c in range(NC):
            for m in range(MINE):
                ch = MINE * c + m
                packed[c, PER * m + ROWS * a : PER * m + ROWS * (a + 1), :] = stage[
                    a, ROWS * ch : ROWS * (ch + 1), :
                ].astype(BF16)
    for k in range(1, NC):
        copy(k).start()
    for k in range(1, NH):
        w_copy(k).start()
    own = pltpu.make_async_copy(packed.at[me_c], got.at[me_c], own_sem.at[0])
    own_far = pltpu.make_async_copy(far_mine, far_got.at[me_c], own_sem.at[1])
    own_w = pltpu.make_async_copy(w_ref, w_got.at[me_h], own_sem.at[2])
    for c in (own, own_far, own_w):
        c.start()
    for c in (own, own_far, own_w):
        c.wait()
    for k in range(1, NC):
        far_copy(k).wait()
        copy(k).wait()
    for k in range(1, NH):
        w_copy(k).wait()


def shifted_taps(taps, big):
    lane = lax.broadcasted_iota(jnp.int32, (16, LANES), 1)
    keep = lane >= lax.broadcasted_iota(jnp.int32, (16, LANES), 0)
    big[0] = jnp.zeros((LANES, LANES), BF16)

    def step(p, carry):
        before, edges = carry
        row = jnp.broadcast_to(taps[pl.ds(p, 1), :], (16, LANES))
        turned = pltpu.roll(row, 0, 1, stride=1, stride_axis=0)
        edge = jnp.where(keep, turned, before).astype(BF16)
        big[p + 1, 0:16, :] = edge
        rolled = []
        for k in range(1, 8):
            r = pltpu.roll(edge, 16 * k, 1)
            big[p + 1, 16 * k : 16 * k + 16, :] = jnp.where(lane >= 16 * k, r, edges[k - 1])
            rolled.append(r)
        return turned, tuple(rolled)

    zero = jnp.zeros((16, LANES), F32)
    lax.fori_loop(0, PIECES, step, (zero, (zero.astype(BF16),) * 7), unroll=16)


def conv_kernel(got, far_got, skip_ref, out, taps, padded, wide, mixed, masks, source, big):
    me_c = lax.axis_index("ctx")
    for d in range(BLOCKS):
        block = lax.broadcasted_iota(jnp.int32, (BLOCKS, LANES), 0)
        mask = jnp.full((BLOCKS, LANES), 1.0 if d < WIN else 0.0, F32)
        if d >= WIN:
            for k in range(4):
                mask = jnp.where(far_got[pl.ds(k, BLOCKS, stride=4), :] == block - d, 1.0, mask)
        masks[d] = mask
    for b in range(SUBS):
        padded[b, 0:BLOCKS, :] = jnp.zeros((BLOCKS, LANES), F32)
    for b in range(4):
        source[BLOCKS, b] = jnp.zeros((BLOCKS, 256), BF16)

    def channel(m, _):
        for c in range(NC):
            base = pl.multiple_of(m * PER, 16)
            taps[ROWS * c : ROWS * (c + 1), :] = got[c, pl.ds(base, 16), :].astype(F32)
            wide[ROWS * c : ROWS * (c + 1), :] = got[c, pl.ds(base + 16, 16), :].astype(F32)
        for b in range(SUBS):
            padded[b, BLOCKS : 2 * BLOCKS, :] = wide[pl.ds(b, BLOCKS, stride=SUBS), :]
        for d in range(BLOCKS):
            mask = masks[d]
            for b in range(SUBS):
                lo = LANES * (b % 2)
                source[d, b // 2, :, lo : lo + LANES] = (
                    padded[b, BLOCKS - d : 2 * BLOCKS - d, :] * mask
                ).astype(BF16)
        shifted_taps(taps, big)

        def group(q4, acc):
            for u in range(4):
                rows = []
                for a in range(4):
                    b = (a - u) % 4
                    rows.append(source[q4 + (u - a + b) // 4, b])
                q = 4 * q4 + u
                here, after, before = big[2 * q + 1], big[2 * q + 2], big[2 * q]
                right = jnp.concatenate(
                    [
                        jnp.concatenate([here, after], axis=1),
                        jnp.concatenate([before, here], axis=1),
                    ],
                    axis=0,
                )
                acc = acc + jnp.dot(
                    jnp.concatenate(rows, axis=0), right, preferred_element_type=F32
                )
            return acc

        acc = lax.fori_loop(0, BLOCKS, group, jnp.zeros((64, 256), F32), unroll=2)
        for c in range(NC):
            base = pl.multiple_of(m * PER, 16)
            wide[ROWS * c : ROWS * (c + 1), :] = got[c, pl.ds(base + 32, 16), :].astype(F32)
        skip = skip_ref[MINE * me_c + m]
        for b in range(SUBS):
            a, lo = b // 2, LANES * (b % 2)
            y = acc[16 * a : 16 * a + 16, lo : lo + LANES] + skip * padded[b, BLOCKS : 2 * BLOCKS, :]
            mixed[pl.ds(b, BLOCKS, stride=SUBS), :] = wide[pl.ds(b, BLOCKS, stride=SUBS), :] * y
        for c in range(NC):
            out[c, pl.ds(pl.multiple_of(m * ROWS, 16), ROWS), :] = mixed[
                ROWS * c : ROWS * (c + 1), :
            ].astype(BF16)
        return 0

    lax.fori_loop(0, MINE, channel, 0)


def project_kernel(
    mixed, w, out, got, stage, sliced, part, result,
    m_send, m_recv, t_send, t_recv, o_send, o_recv, own_sem,
):
    me_c, me_h = lax.axis_index("ctx"), lax.axis_index("head")
    greet(me_c, me_h)

    def m_copy(k):
        peer = lax.rem(me_c + k, NC)
        return pltpu.make_async_remote_copy(
            src_ref=mixed.at[peer], dst_ref=got.at[me_c], send_sem=m_send.at[k], recv_sem=m_recv.at[k],
            device_id={"ctx": peer}, device_id_type=MESH,
        )

    def t_copy(k):
        peer = lax.rem(me_h + k, NH)
        return pltpu.make_async_remote_copy(
            src_ref=sliced.at[peer], dst_ref=part.at[me_h], send_sem=t_send.at[k], recv_sem=t_recv.at[k],
            device_id={"head": peer}, device_id_type=MESH,
        )

    def o_copy(k):
        peer = lax.rem(me_h + k, NH)
        return pltpu.make_async_remote_copy(
            src_ref=result.at[peer],
            dst_ref=out.at[:, pl.ds(pl.multiple_of(me_h * LANES, LANES), LANES)],
            send_sem=o_send.at[k], recv_sem=o_recv.at[k],
            device_id={"head": peer}, device_id_type=MESH,
        )

    for k in range(1, NC):
        m_copy(k).start()
    own = pltpu.make_async_copy(mixed.at[me_c], got.at[me_c], own_sem.at[0])
    own.start()
    own.wait()
    for k in range(1, NC):
        m_copy(k).wait()
    for c in range(NC):
        stage[64 * c : 64 * c + 64, :] = got[c].astype(F32)
    for t in range(NH):
        sliced[t] = stage[pl.ds(t, CH, stride=NH), :].astype(BF16)
    for k in range(1, NH):
        t_copy(k).start()
    own = pltpu.make_async_copy(sliced.at[me_h], part.at[me_h], own_sem.at[1])
    own.start()
    own.wait()
    for k in range(1, NH):
        t_copy(k).wait()
    total = lax.dot_general(
        w[...].reshape(NH * CH, NH * CH), part[...].reshape(NH * CH, LANES),
        (((0,), (0,)), ((), ())), preferred_element_type=F32,
    )
    for t in range(NH):
        result[t] = total[CH * t : CH * (t + 1), :]
    for k in range(1, NH):
        o_copy(k).start()
    own = pltpu.make_async_copy(
        result.at[me_h], out.at[:, pl.ds(pl.multiple_of(me_h * LANES, LANES), LANES)], own_sem.at[2]
    )
    own.start()
    own.wait()
    for k in range(1, NH):
        o_copy(k).wait()


def local(inputs, gate, filter_taps, skip, w_out, far_pairs):
    vmem = pl.BlockSpec(memory_space=pltpu.VMEM)
    smem = pl.BlockSpec(memory_space=pltpu.SMEM)
    dma = pltpu.SemaphoreType.DMA
    got, far_got, w_all = pl.pallas_call(
        spread_kernel,
        out_shape=[
            jax.ShapeDtypeStruct((NC, MINE * PER, LANES), BF16),
            jax.ShapeDtypeStruct((NC, 8, LANES), jnp.int32),
            jax.ShapeDtypeStruct((NH, CH, NH * CH), BF16),
        ],
        in_specs=[vmem] * 4 + [smem],
        out_specs=[vmem] * 3,
        scratch_shapes=[
            pltpu.VMEM((3, CH * ROWS, LANES), F32),
            pltpu.VMEM((NC, MINE * PER, LANES), BF16),
            pltpu.VMEM((8, LANES), jnp.int32),
            dma((NC,)), dma((NC,)), dma((NC,)), dma((NC,)), dma((NH,)), dma((NH,)), dma((3,)),
        ],
        compiler_params=pltpu.CompilerParams(
            collective_id=0, has_side_effects=True, vmem_limit_bytes=40 << 20
        ),
    )(inputs, gate, filter_taps, w_out, far_pairs)
    mixed = pl.pallas_call(
        conv_kernel,
        out_shape=jax.ShapeDtypeStruct((NC, MINE * ROWS, LANES), BF16),
        in_specs=[vmem, vmem, smem],
        out_specs=vmem,
        scratch_shapes=[
            pltpu.VMEM((PIECES, LANES), F32),
            pltpu.VMEM((SUBS, 2 * BLOCKS, LANES), F32),
            pltpu.VMEM((PIECES, LANES), F32),
            pltpu.VMEM((PIECES, LANES), F32),
            pltpu.VMEM((BLOCKS, BLOCKS, LANES), F32),
            pltpu.VMEM((BLOCKS + 1, 4, BLOCKS, 256), BF16),
            pltpu.VMEM((PIECES + 1, LANES, LANES), BF16),
        ],
        compiler_params=pltpu.CompilerParams(vmem_limit_bytes=40 << 20),
    )(got, far_got.reshape(NC * 8, LANES), skip)
    return pl.pallas_call(
        project_kernel,
        out_shape=jax.ShapeDtypeStruct((CH, NH * LANES), F32),
        in_specs=[vmem, vmem],
        out_specs=vmem,
        scratch_shapes=[
            pltpu.VMEM((NC, MINE * ROWS, LANES), BF16),
            pltpu.VMEM((CH * ROWS, LANES), F32),
            pltpu.VMEM((NH, CH, LANES), BF16),
            pltpu.VMEM((NH, CH, LANES), BF16),
            pltpu.VMEM((NH, CH, LANES), F32),
            dma((NC,)), dma((NC,)), dma((NH,)), dma((NH,)), dma((NH,)), dma((NH,)), dma((3,)),
        ],
        compiler_params=pltpu.CompilerParams(
            collective_id=1, has_side_effects=True, vmem_limit_bytes=40 << 20
        ),
    )(mixed, w_all)


def solution(mesh):
    in_specs = (
        P("head", "ctx"),
        P("head", "ctx"),
        P("head", "ctx"),
        P("head"),
        P("head", None),
        P("ctx", None),
    )
    out_specs = P("head", "ctx")
    return jax.shard_map(local, mesh=mesh, in_specs=in_specs, out_specs=out_specs, check_vma=False)
```

```python
import jax
import jax.numpy as jnp
from jax import lax
from jax.experimental import pallas as pl
from jax.experimental.pallas import tpu as pltpu
from jax.sharding import PartitionSpec as P

F32 = jnp.float32
BF16 = jnp.bfloat16
LANES = 128
BLOCKS = 16
SUBS = 8
PIECES = BLOCKS * SUBS
NC = 8
NH = 16
CH = 32
MINE = CH // NC
ROWS = 16
PER = 3 * ROWS
WIN = 2
MESH = pl.DeviceIdType.MESH


def greet(me_c, me_h):
    barrier = pltpu.get_barrier_semaphore()
    for k in range(1, NC):
        pl.semaphore_signal(
            barrier, inc=1, device_id={"ctx": lax.rem(me_c + k, NC)}, device_id_type=MESH
        )
    for k in range(1, NH):
        pl.semaphore_signal(
            barrier, inc=1, device_id={"head": lax.rem(me_h + k, NH)}, device_id_type=MESH
        )


def shifted_taps(taps, big):
    lane = lax.broadcasted_iota(jnp.int32, (16, LANES), 1)
    keep = lane >= lax.broadcasted_iota(jnp.int32, (16, LANES), 0)
    big[0] = jnp.zeros((LANES, LANES), BF16)

    def step(p, carry):
        before, edges = carry
        row = jnp.broadcast_to(taps[pl.ds(p, 1), :], (16, LANES))
        turned = pltpu.roll(row, 0, 1, stride=1, stride_axis=0)
        edge = jnp.where(keep, turned, before).astype(BF16)
        big[p + 1, 0:16, :] = edge
        rolled = []
        for k in range(1, 8):
            r = pltpu.roll(edge, 16 * k, 1)
            big[p + 1, 16 * k : 16 * k + 16, :] = jnp.where(lane >= 16 * k, r, edges[k - 1])
            rolled.append(r)
        return turned, tuple(rolled)

    zero = jnp.zeros((16, LANES), F32)
    lax.fori_loop(0, PIECES, step, (zero, (zero.astype(BF16),) * 7), unroll=16)


def fill(me_c, m, got, lo, wide):
    for c in range(NC):
        base = pl.multiple_of(m * PER + lo, 16)
        wide[ROWS * c : ROWS * (c + 1), :] = got[c, pl.ds(base, ROWS), :].astype(F32)


def kernel(
    x_hbm, g_hbm, h_hbm, w_hbm, far_hbm, skip_hbm, out,
    x_in, g_in, h_in, w_in, far_in, skip_in,
    stage, packed, got, far_mine, far_got, w_got,
    taps, padded, wide, mixed, masks, source, big,
    ready, back, regroup, sliced, part, result,
    load_sem, own_sem, in_send, in_recv, far_send, far_recv, w_send, w_recv,
    m_send, m_recv, t_send, t_recv, o_send, o_recv,
):
    me_c, me_h = lax.axis_index("ctx"), lax.axis_index("head")

    def remote(src, dst, send, recv, axis, k):
        me, n = (me_c, NC) if axis == "ctx" else (me_h, NH)
        return pltpu.make_async_remote_copy(
            src_ref=src, dst_ref=dst, send_sem=send, recv_sem=recv,
            device_id={axis: lax.rem(me + k, n)}, device_id_type=MESH,
        )

    def far_copy(k):
        return remote(far_mine, far_got.at[me_c], far_send.at[k], far_recv.at[k], "ctx", k)

    def w_copy(k):
        return remote(w_in, w_got.at[me_h], w_send.at[k], w_recv.at[k], "head", k)

    def in_copy(m, k):
        rows = pl.ds(pl.multiple_of(m * PER, 16), PER)
        peer = lax.rem(me_c + k, NC)
        return remote(
            packed.at[peer, rows], got.at[me_c, rows], in_send.at[m, k], in_recv.at[m, k], "ctx", k
        )

    def m_copy(m, k):
        rows = pl.ds(pl.multiple_of(m * ROWS, 16), ROWS)
        peer = lax.rem(me_c + k, NC)
        return remote(
            ready.at[peer, rows], back.at[me_c, rows], m_send.at[m, k], m_recv.at[m, k], "ctx", k
        )

    def t_copy(k):
        peer = lax.rem(me_h + k, NH)
        return remote(sliced.at[peer], part.at[me_h], t_send.at[k], t_recv.at[k], "head", k)

    columns = pl.ds(pl.multiple_of(me_h * LANES, LANES), LANES)

    def o_copy(k):
        peer = lax.rem(me_h + k, NH)
        return remote(result.at[peer], out.at[:, columns], o_send.at[k], o_recv.at[k], "head", k)

    loads = [
        pltpu.make_async_copy(a, b, load_sem.at[i])
        for i, (a, b) in enumerate(
            (
                (h_hbm, h_in), (x_hbm, x_in), (g_hbm, g_in), (far_hbm, far_in),
                (skip_hbm, skip_in), (w_hbm, w_in),
            )
        )
    ]
    for copy in loads:
        copy.start()
    greet(me_c, me_h)
    for copy in loads:
        copy.wait()
    row = lax.broadcasted_iota(jnp.int32, (8, LANES), 0)
    table = jnp.full((8, LANES), -1, jnp.int32)
    for r in range(2):
        for k in range(4):
            table = jnp.where(row == 4 * r + k, far_in[r, k], table)
    far_mine[...] = table
    for a, ref in enumerate((h_in, x_in, g_in)):
        for s in range(ROWS):
            stage[a, pl.ds(s, CH, stride=ROWS), :] = ref[:, LANES * s : LANES * (s + 1)].astype(F32)
        for c in range(NC):
            for m in range(MINE):
                ch = MINE * c + m
                packed[c, PER * m + ROWS * a : PER * m + ROWS * (a + 1), :] = stage[
                    a, ROWS * ch : ROWS * (ch + 1), :
                ].astype(BF16)
    pl.semaphore_wait(pltpu.get_barrier_semaphore(), NC - 1 + NH - 1)

    for k in range(1, NC):
        far_copy(k).start()
    for m in range(MINE):
        for k in range(1, NC):
            in_copy(m, k).start()
    for k in range(1, NH):
        w_copy(k).start()
    own = [
        pltpu.make_async_copy(a, b, own_sem.at[i])
        for i, (a, b) in enumerate(
            (
                (far_mine, far_got.at[me_c]), (packed.at[me_c], got.at[me_c]), (w_in, w_got.at[me_h]),
            )
        )
    ]
    for copy in own:
        copy.start()
    for copy in own:
        copy.wait()
    for b in range(SUBS):
        padded[b, 0:BLOCKS, :] = jnp.zeros((BLOCKS, LANES), F32)
    for b in range(4):
        source[BLOCKS, b] = jnp.zeros((BLOCKS, 256), BF16)
    for k in range(1, NC):
        far_copy(k).wait()
    for c in range(NC):
        regroup[8 * c : 8 * c + 8, :] = far_got[c]
    for d in range(BLOCKS):
        block = lax.broadcasted_iota(jnp.int32, (BLOCKS, LANES), 0)
        mask = jnp.full((BLOCKS, LANES), 1.0 if d < WIN else 0.0, F32)
        if d >= WIN:
            for k in range(4):
                mask = jnp.where(regroup[pl.ds(k, BLOCKS, stride=4), :] == block - d, 1.0, mask)
        masks[d] = mask

    def channel(m, _):
        for k in range(1, NC):
            in_copy(m, k).wait()
        fill(me_c, m, got, 0, taps)
        fill(me_c, m, got, ROWS, wide)
        for b in range(SUBS):
            padded[b, BLOCKS : 2 * BLOCKS, :] = wide[pl.ds(b, BLOCKS, stride=SUBS), :]
        for d in range(BLOCKS):
            mask = masks[d]
            for b in range(SUBS):
                lo = LANES * (b % 2)
                source[d, b // 2, :, lo : lo + LANES] = (
                    padded[b, BLOCKS - d : 2 * BLOCKS - d, :] * mask
                ).astype(BF16)
        shifted_taps(taps, big)

        def group(q4, acc):
            for u in range(4):
                rows = []
                for a in range(4):
                    b = (a - u) % 4
                    rows.append(source[q4 + (u - a + b) // 4, b])
                q = 4 * q4 + u
                here, after, before = big[2 * q + 1], big[2 * q + 2], big[2 * q]
                right = jnp.concatenate(
                    [
                        jnp.concatenate([here, after], axis=1),
                        jnp.concatenate([before, here], axis=1),
                    ],
                    axis=0,
                )
                acc = acc + jnp.dot(
                    jnp.concatenate(rows, axis=0), right, preferred_element_type=F32
                )
            return acc

        acc = lax.fori_loop(0, BLOCKS, group, jnp.zeros((64, 256), F32), unroll=2)
        fill(me_c, m, got, 2 * ROWS, wide)
        skip = skip_in[MINE * me_c + m]
        for b in range(SUBS):
            a, lo = b // 2, LANES * (b % 2)
            y = acc[16 * a : 16 * a + 16, lo : lo + LANES] + skip * padded[b, BLOCKS : 2 * BLOCKS, :]
            mixed[pl.ds(b, BLOCKS, stride=SUBS), :] = wide[pl.ds(b, BLOCKS, stride=SUBS), :] * y
        for c in range(NC):
            ready[c, pl.ds(pl.multiple_of(m * ROWS, 16), ROWS), :] = mixed[
                ROWS * c : ROWS * (c + 1), :
            ].astype(BF16)
        for k in range(1, NC):
            m_copy(m, k).start()
        return 0

    lax.fori_loop(0, MINE, channel, 0)
    copy = pltpu.make_async_copy(ready.at[me_c], back.at[me_c], own_sem.at[3])
    copy.start()
    copy.wait()
    for m in range(MINE):
        for k in range(1, NC):
            m_copy(m, k).wait()
    for c in range(NC):
        stage[0, 64 * c : 64 * c + 64, :] = back[c].astype(F32)
    for t in range(NH):
        sliced[t] = stage[0, pl.ds(t, CH, stride=NH), :].astype(BF16)
    for k in range(1, NH):
        t_copy(k).start()
    copy = pltpu.make_async_copy(sliced.at[me_h], part.at[me_h], own_sem.at[4])
    copy.start()
    copy.wait()
    for k in range(1, NH):
        w_copy(k).wait()
    for k in range(1, NH):
        t_copy(k).wait()
    total = lax.dot_general(
        w_got[...].reshape(NH * CH, NH * CH), part[...].reshape(NH * CH, LANES),
        (((0,), (0,)), ((), ())), preferred_element_type=F32,
    )
    for t in range(NH):
        result[t] = total[CH * t : CH * (t + 1), :]
    for k in range(1, NH):
        o_copy(k).start()
    copy = pltpu.make_async_copy(result.at[me_h], out.at[:, columns], own_sem.at[5])
    copy.start()
    copy.wait()
    for k in range(1, NH):
        o_copy(k).wait()


def local(inputs, gate, filter_taps, skip, w_out, far_pairs):
    hbm = pl.BlockSpec(memory_space=pltpu.HBM)
    dma = pltpu.SemaphoreType.DMA
    vmem = pltpu.VMEM
    return pl.pallas_call(
        kernel,
        out_shape=jax.ShapeDtypeStruct((CH, NH * LANES), F32),
        in_specs=[hbm] * 6,
        out_specs=hbm,
        scratch_shapes=[
            vmem(inputs.shape, BF16), vmem(gate.shape, BF16), vmem(filter_taps.shape, F32),
            vmem(w_out.shape, BF16), pltpu.SMEM(far_pairs.shape, jnp.int32), pltpu.SMEM(skip.shape, F32),
            vmem((3, CH * ROWS, LANES), F32),
            vmem((NC, MINE * PER, LANES), BF16),
            vmem((NC, MINE * PER, LANES), BF16),
            vmem((8, LANES), jnp.int32),
            vmem((NC, 8, LANES), jnp.int32),
            vmem((NH, CH, NH * CH), BF16),
            vmem((PIECES, LANES), F32),
            vmem((SUBS, 2 * BLOCKS, LANES), F32),
            vmem((PIECES, LANES), F32),
            vmem((PIECES, LANES), F32),
            vmem((BLOCKS, BLOCKS, LANES), F32),
            vmem((BLOCKS + 1, 4, BLOCKS, 256), BF16),
            vmem((PIECES + 1, LANES, LANES), BF16),
            vmem((NC, MINE * ROWS, LANES), BF16),
            vmem((NC, MINE * ROWS, LANES), BF16),
            vmem((NC * 8, LANES), jnp.int32),
            vmem((NH, CH, LANES), BF16),
            vmem((NH, CH, LANES), BF16),
            vmem((NH, CH, LANES), F32),
            dma((6,)), dma((6,)), dma((MINE, NC)), dma((MINE, NC)), dma((NC,)), dma((NC,)),
            dma((NH,)), dma((NH,)), dma((MINE, NC)), dma((MINE, NC)),
            dma((NH,)), dma((NH,)), dma((NH,)), dma((NH,)),
        ],
        compiler_params=pltpu.CompilerParams(
            collective_id=0, has_side_effects=True, vmem_limit_bytes=40 << 20
        ),
    )(inputs, gate, filter_taps, w_out, far_pairs, skip)


def solution(mesh):
    in_specs = (
        P("head", "ctx"),
        P("head", "ctx"),
        P("head", "ctx"),
        P("head"),
        P("head", None),
        P("ctx", None),
    )
    out_specs = P("head", "ctx")
    return jax.shard_map(local, mesh=mesh, in_specs=in_specs, out_specs=out_specs, check_vma=False)
```

```python
import jax
import jax.numpy as jnp
from jax import lax
from jax.experimental import pallas as pl
from jax.experimental.pallas import tpu as pltpu
from jax.sharding import PartitionSpec as P

F32 = jnp.float32
BF16 = jnp.bfloat16
LANES = 128
BLOCKS = 16
SUBS = 8
PIECES = BLOCKS * SUBS
NC = 8
NH = 16
CH = 32
MINE = CH // NC
ROWS = 16
PER = 3 * ROWS
WIN = 2
PART = 16
TILES = 5
MESH = pl.DeviceIdType.MESH


def greet(me_c, me_h):
    barrier = pltpu.get_barrier_semaphore()
    for k in range(1, NC):
        pl.semaphore_signal(
            barrier, inc=1, device_id={"ctx": lax.rem(me_c + k, NC)}, device_id_type=MESH
        )
    for k in range(1, NH):
        pl.semaphore_signal(
            barrier, inc=1, device_id={"head": lax.rem(me_h + k, NH)}, device_id_type=MESH
        )


def read_masks(far, masks):
    block = lax.broadcasted_iota(jnp.int32, (BLOCKS, LANES), 0)
    chunk = lax.broadcasted_iota(jnp.int32, (BLOCKS, LANES), 1) // PART

    def reads(lag):
        if lag < WIN:
            return jnp.ones((BLOCKS, LANES), F32)
        mask = jnp.zeros((BLOCKS, LANES), F32)
        if lag < BLOCKS:
            for k in range(4):
                mask = jnp.where(far[pl.ds(k, BLOCKS, stride=4), :] == block - lag, 1.0, mask)
        return mask

    now = reads(0)
    for d in range(BLOCKS):
        after = reads(d + 1)
        masks[0, d] = after
        for a in range(1, TILES - 1):
            masks[a, d] = jnp.where(chunk <= 2 * a - 1, now, after)
        masks[TILES - 1, d] = now
        now = after


def prepare(m, read, taps, wide, turned, base, edges):
    read(m, 1, wide)
    read(m, 0, taps)
    lane = lax.broadcasted_iota(jnp.int32, (PART, LANES), 1)
    chunk = lane // PART
    for b in range(SUBS):
        piece = wide[pl.ds(b, BLOCKS, stride=SUBS), :]
        for s in range(SUBS):
            turned[b, s, BLOCKS : 2 * BLOCKS, :] = pltpu.roll(piece, PART * s, 1) if s else piece
    for f in range(SUBS):
        for a in range(TILES):
            tile = None
            for v in range(SUBS):
                b = 2 * a - 1 - v
                lo = BLOCKS if b >= 0 else BLOCKS - 1
                piece = turned[b % SUBS, (v - f) % SUBS, lo : lo + BLOCKS, :]
                tile = piece if tile is None else jnp.where(chunk == v, piece, tile)
            base[f, a, BLOCKS : 2 * BLOCKS, :] = tile
    keep = lane >= lax.broadcasted_iota(jnp.int32, (PART, LANES), 0)
    before = jnp.zeros((PART, LANES), F32)
    for p in range(PIECES):
        row = jnp.broadcast_to(taps[p : p + 1, :], (PART, LANES))
        turn = pltpu.roll(row, 0, 1, stride=1, stride_axis=0)
        edges[PART * (p + 1) : PART * (p + 2), :] = jnp.where(keep, turn, before).astype(BF16)
        before = turn


def multiply(masks, base, edges, total):
    for g in range(0, BLOCKS, 2):
        left = []
        for f in range(SUBS):
            for a in range(TILES):
                left.append(
                    jnp.concatenate(
                        [
                            (base[f, a, BLOCKS - d : 2 * BLOCKS - d, :] * masks[a, d]).astype(BF16)
                            for d in (g, g + 1)
                        ],
                        axis=1,
                    )
                )
        lo = LANES * g
        right = jnp.concatenate(
            [edges[lo : lo + 256, :], edges[lo + PART : lo + PART + 256, :]], axis=1
        )
        part = jnp.dot(jnp.concatenate(left, axis=0), right, preferred_element_type=F32)
        if g == 0:
            total[...] = part
        else:
            total[...] += part


def finish(m, read, skip, total, wide, gate, mixed):
    read(m, 2, gate)
    read(m, 1, wide)
    lane = lax.broadcasted_iota(jnp.int32, (BLOCKS, LANES), 1)
    for a in range(TILES - 1):
        for f in range(SUBS):
            row = BLOCKS * (TILES * f + a + 1)
            first = total[row : row + BLOCKS, 0:LANES]
            second = total[row : row + BLOCKS, LANES : 2 * LANES]
            if f == 0:
                low, high = first, second
                continue
            before = pltpu.roll(total[row - BLOCKS : row, LANES : 2 * LANES], PART * f, 1)
            first, second = pltpu.roll(first, PART * f, 1), pltpu.roll(second, PART * f, 1)
            low = low + jnp.where(lane >= PART * f, first, before)
            high = high + jnp.where(lane >= PART * f, second, first)
        for b, y in ((2 * a, low), (2 * a + 1, high)):
            rows = pl.ds(b, BLOCKS, stride=SUBS)
            mixed[rows, :] = gate[rows, :] * (y + skip * wide[rows, :])


def kernel(
    x_hbm, g_hbm, h_hbm, w_hbm, far_hbm, skip_hbm, out,
    x_in, g_in, h_in, w_in, far_in, skip_in,
    stage, packed, got, far_mine, far_got, w_got,
    taps, wide, x_own, g_own, mixed, masks, turned, base0, edges0, total0, base1, edges1, total1,
    ready, back, regroup, sliced, part, result,
    load_sem, own_sem, in_send, in_recv, far_send, far_recv, w_send, w_recv,
    m_send, m_recv, t_send, t_recv, o_send, o_recv,
):
    me_c, me_h = lax.axis_index("ctx"), lax.axis_index("head")

    def remote(src, dst, send, recv, axis, k):
        me, n = (me_c, NC) if axis == "ctx" else (me_h, NH)
        return pltpu.make_async_remote_copy(
            src_ref=src, dst_ref=dst, send_sem=send, recv_sem=recv,
            device_id={axis: lax.rem(me + k, n)}, device_id_type=MESH,
        )

    def far_copy(k):
        return remote(far_mine, far_got.at[me_c], far_send.at[k], far_recv.at[k], "ctx", k)

    def w_copy(k):
        return remote(w_in, w_got.at[me_h], w_send.at[k], w_recv.at[k], "head", k)

    def in_copy(m, k):
        rows = pl.ds(pl.multiple_of(m * PER, 16), PER)
        peer = lax.rem(me_c + k, NC)
        return remote(
            packed.at[peer, rows], got.at[me_c, rows], in_send.at[m, k], in_recv.at[m, k], "ctx", k
        )

    def m_copy(m, k):
        rows = pl.ds(pl.multiple_of(m * ROWS, 16), ROWS)
        peer = lax.rem(me_c + k, NC)
        return remote(
            ready.at[peer, rows], back.at[me_c, rows], m_send.at[m, k], m_recv.at[m, k], "ctx", k
        )

    def t_copy(k):
        peer = lax.rem(me_h + k, NH)
        return remote(sliced.at[peer], part.at[me_h], t_send.at[k], t_recv.at[k], "head", k)

    columns = pl.ds(pl.multiple_of(me_h * LANES, LANES), LANES)

    def o_copy(k):
        peer = lax.rem(me_h + k, NH)
        return remote(result.at[peer], out.at[:, columns], o_send.at[k], o_recv.at[k], "head", k)

    loads = [
        pltpu.make_async_copy(a, b, load_sem.at[i])
        for i, (a, b) in enumerate(
            (
                (h_hbm, h_in), (x_hbm, x_in), (g_hbm, g_in), (far_hbm, far_in),
                (skip_hbm, skip_in), (w_hbm, w_in),
            )
        )
    ]
    for copy in loads:
        copy.start()
    greet(me_c, me_h)
    for copy in loads:
        copy.wait()
    row = lax.broadcasted_iota(jnp.int32, (8, LANES), 0)
    table = jnp.full((8, LANES), -1, jnp.int32)
    for r in range(2):
        for k in range(4):
            table = jnp.where(row == 4 * r + k, far_in[r, k], table)
    far_mine[...] = table
    for a, ref in enumerate((h_in, x_in, g_in)):
        for s in range(ROWS):
            stage[a, pl.ds(s, CH, stride=ROWS), :] = ref[:, LANES * s : LANES * (s + 1)].astype(F32)
        for c in range(NC):
            for m in range(MINE):
                ch = MINE * c + m
                packed[c, PER * m + ROWS * a : PER * m + ROWS * (a + 1), :] = stage[
                    a, ROWS * ch : ROWS * (ch + 1), :
                ].astype(BF16)
    pl.semaphore_wait(pltpu.get_barrier_semaphore(), NC - 1 + NH - 1)

    for k in range(1, NC):
        far_copy(k).start()
    for m in range(MINE):
        for k in range(1, NC):
            in_copy(m, k).start()
    for k in range(1, NH):
        w_copy(k).start()
    own = [
        pltpu.make_async_copy(a, b, own_sem.at[i])
        for i, (a, b) in enumerate(
            (
                (far_mine, far_got.at[me_c]), (packed.at[me_c], got.at[me_c]), (w_in, w_got.at[me_h]),
            )
        )
    ]
    for copy in own:
        copy.start()
    for copy in own:
        copy.wait()
    empty = jnp.zeros((BLOCKS, LANES), F32)
    for f in range(SUBS):
        for a in range(TILES):
            base0[f, a, 0:BLOCKS, :] = empty
            base1[f, a, 0:BLOCKS, :] = empty
        for b in range(SUBS):
            turned[b, f, 0:BLOCKS, :] = empty
    edges0[0:PART, :] = empty.astype(BF16)
    edges1[0:PART, :] = empty.astype(BF16)
    for k in range(1, NC):
        far_copy(k).wait()
    for c in range(NC):
        regroup[8 * c : 8 * c + 8, :] = far_got[c]
    read_masks(regroup, masks)

    def read(m, a, to):
        rows = pl.ds(pl.multiple_of(m * PER + a * ROWS, 16), ROWS)
        for c in range(NC):
            to[ROWS * c : ROWS * (c + 1), :] = got[c, rows, :].astype(F32)

    def arrive(m):
        for k in range(1, NC):
            in_copy(m, k).wait()

    def hand_back(m, total):
        finish(m, read, skip_in[MINE * me_c + m], total, x_own, g_own, mixed)
        for c in range(NC):
            ready[c, pl.ds(pl.multiple_of(m * ROWS, 16), ROWS), :] = mixed[
                ROWS * c : ROWS * (c + 1), :
            ].astype(BF16)

    def send_back(m):
        for k in range(1, NC):
            m_copy(m, k).start()

    arrive(0)
    prepare(0, read, taps, wide, turned, base0, edges0)

    def pair(t, _):
        arrive(2 * t + 1)
        multiply(masks, base0, edges0, total0)
        prepare(2 * t + 1, read, taps, wide, turned, base1, edges1)

        @pl.when(t == 0)
        def _():
            arrive(2)

        multiply(masks, base1, edges1, total1)
        prepare(jnp.minimum(2 * t + 2, MINE - 1), read, taps, wide, turned, base0, edges0)
        hand_back(2 * t, total0)
        send_back(2 * t)
        hand_back(2 * t + 1, total1)
        send_back(2 * t + 1)
        return 0

    lax.fori_loop(0, MINE // 2, pair, 0)
    copy = pltpu.make_async_copy(ready.at[me_c], back.at[me_c], own_sem.at[3])
    copy.start()
    copy.wait()
    for m in range(MINE):
        for k in range(1, NC):
            m_copy(m, k).wait()
    for c in range(NC):
        stage[0, 64 * c : 64 * c + 64, :] = back[c].astype(F32)
    for t in range(NH):
        sliced[t] = stage[0, pl.ds(t, CH, stride=NH), :].astype(BF16)
    for k in range(1, NH):
        t_copy(k).start()
    copy = pltpu.make_async_copy(sliced.at[me_h], part.at[me_h], own_sem.at[4])
    copy.start()
    copy.wait()
    for k in range(1, NH):
        w_copy(k).wait()
    for k in range(1, NH):
        t_copy(k).wait()
    total = lax.dot_general(
        w_got[...].reshape(NH * CH, NH * CH), part[...].reshape(NH * CH, LANES),
        (((0,), (0,)), ((), ())), preferred_element_type=F32,
    )
    for t in range(NH):
        result[t] = total[CH * t : CH * (t + 1), :]
    for k in range(1, NH):
        o_copy(k).start()
    copy = pltpu.make_async_copy(result.at[me_h], out.at[:, columns], own_sem.at[5])
    copy.start()
    copy.wait()
    for k in range(1, NH):
        o_copy(k).wait()


def local(inputs, gate, filter_taps, skip, w_out, far_pairs):
    hbm = pl.BlockSpec(memory_space=pltpu.HBM)
    dma = pltpu.SemaphoreType.DMA
    vmem = pltpu.VMEM
    return pl.pallas_call(
        kernel,
        out_shape=jax.ShapeDtypeStruct((CH, NH * LANES), F32),
        in_specs=[hbm] * 6,
        out_specs=hbm,
        scratch_shapes=[
            vmem(inputs.shape, BF16), vmem(gate.shape, BF16), vmem(filter_taps.shape, F32),
            vmem(w_out.shape, BF16), pltpu.SMEM(far_pairs.shape, jnp.int32), pltpu.SMEM(skip.shape, F32),
            vmem((3, CH * ROWS, LANES), F32),
            vmem((NC, MINE * PER, LANES), BF16),
            vmem((NC, MINE * PER, LANES), BF16),
            vmem((8, LANES), jnp.int32),
            vmem((NC, 8, LANES), jnp.int32),
            vmem((NH, CH, NH * CH), BF16),
            *[vmem((PIECES, LANES), F32)] * 5,
            vmem((TILES, BLOCKS, BLOCKS, LANES), F32),
            vmem((SUBS, SUBS, 2 * BLOCKS, LANES), F32),
            *[
                vmem((SUBS, TILES, 2 * BLOCKS, LANES), F32),
                vmem((PART * (PIECES + 1), LANES), BF16),
                vmem((SUBS * TILES * BLOCKS, 2 * LANES), F32),
            ]
            * 2,
            vmem((NC, MINE * ROWS, LANES), BF16),
            vmem((NC, MINE * ROWS, LANES), BF16),
            vmem((NC * 8, LANES), jnp.int32),
            vmem((NH, CH, LANES), BF16),
            vmem((NH, CH, LANES), BF16),
            vmem((NH, CH, LANES), F32),
            dma((6,)), dma((6,)), dma((MINE, NC)), dma((MINE, NC)), dma((NC,)), dma((NC,)),
            dma((NH,)), dma((NH,)), dma((MINE, NC)), dma((MINE, NC)),
            dma((NH,)), dma((NH,)), dma((NH,)), dma((NH,)),
        ],
        compiler_params=pltpu.CompilerParams(
            collective_id=0, has_side_effects=True, vmem_limit_bytes=62 << 20
        ),
    )(inputs, gate, filter_taps, w_out, far_pairs, skip)


def solution(mesh):
    in_specs = (
        P("head", "ctx"),
        P("head", "ctx"),
        P("head", "ctx"),
        P("head"),
        P("head", None),
        P("ctx", None),
    )
    out_specs = P("head", "ctx")
    return jax.shard_map(local, mesh=mesh, in_specs=in_specs, out_specs=out_specs, check_vma=False)
```

```python
import jax
import jax.numpy as jnp
from jax import lax
from jax.experimental import pallas as pl
from jax.experimental.pallas import tpu as pltpu
from jax.sharding import PartitionSpec as P

F32 = jnp.float32
BF16 = jnp.bfloat16
LANES = 128
BLOCKS = 16
SUBS = 8
PIECES = BLOCKS * SUBS
NC = 8
NH = 16
CH = 32
MINE = CH // NC
ROWS = 16
PER = 2 * ROWS
GATES = MINE * PER
WIN = 2
PART = 16
TILES = 5
MESH = pl.DeviceIdType.MESH


def greet(me_c, me_h):
    barrier = pltpu.get_barrier_semaphore()
    for k in range(1, NC):
        pl.semaphore_signal(
            barrier, inc=1, device_id={"ctx": lax.rem(me_c + k, NC)}, device_id_type=MESH
        )
    for k in range(1, NH):
        pl.semaphore_signal(
            barrier, inc=1, device_id={"head": lax.rem(me_h + k, NH)}, device_id_type=MESH
        )


def read_masks(far, masks):
    block = lax.broadcasted_iota(jnp.int32, (BLOCKS, LANES), 0)
    chunk = lax.broadcasted_iota(jnp.int32, (BLOCKS, LANES), 1) // PART

    def reads(lag):
        if lag < WIN:
            return jnp.ones((BLOCKS, LANES), F32)
        mask = jnp.zeros((BLOCKS, LANES), F32)
        if lag < BLOCKS:
            for k in range(4):
                mask = jnp.where(far[pl.ds(k, BLOCKS, stride=4), :] == block - lag, 1.0, mask)
        return mask

    now = reads(0)
    for d in range(BLOCKS):
        after = reads(d + 1)
        masks[0, d] = after
        for a in range(1, TILES - 1):
            masks[a, d] = jnp.where(chunk <= 2 * a - 1, now, after)
        masks[TILES - 1, d] = now
        now = after


def prepare(m, read, taps, wide, turned, base, edges):
    read(m, 1, wide)
    read(m, 0, taps)
    lane = lax.broadcasted_iota(jnp.int32, (PART, LANES), 1)
    chunk = lane // PART
    for b in range(SUBS):
        piece = wide[pl.ds(b, BLOCKS, stride=SUBS), :]
        for s in range(SUBS):
            turned[b, s, BLOCKS : 2 * BLOCKS, :] = pltpu.roll(piece, PART * s, 1) if s else piece
    for f in range(SUBS):
        for a in range(TILES):
            tile = None
            for v in range(SUBS):
                b = 2 * a - 1 - v
                lo = BLOCKS if b >= 0 else BLOCKS - 1
                piece = turned[b % SUBS, (v - f) % SUBS, lo : lo + BLOCKS, :]
                tile = piece if tile is None else jnp.where(chunk == v, piece, tile)
            base[f, a, BLOCKS : 2 * BLOCKS, :] = tile
    keep = lane >= lax.broadcasted_iota(jnp.int32, (PART, LANES), 0)
    before = jnp.zeros((PART, LANES), F32)
    for p in range(PIECES):
        row = jnp.broadcast_to(taps[p : p + 1, :], (PART, LANES))
        turn = pltpu.roll(row, 0, 1, stride=1, stride_axis=0)
        edges[PART * (p + 1) : PART * (p + 2), :] = jnp.where(keep, turn, before).astype(BF16)
        before = turn


def multiply(masks, base, edges, total):
    for g in range(0, BLOCKS, 2):
        left = []
        for f in range(SUBS):
            for a in range(TILES):
                left.append(
                    jnp.concatenate(
                        [
                            (base[f, a, BLOCKS - d : 2 * BLOCKS - d, :] * masks[a, d]).astype(BF16)
                            for d in (g, g + 1)
                        ],
                        axis=1,
                    )
                )
        lo = LANES * g
        right = jnp.concatenate(
            [edges[lo : lo + 256, :], edges[lo + PART : lo + PART + 256, :]], axis=1
        )
        part = jnp.dot(jnp.concatenate(left, axis=0), right, preferred_element_type=F32)
        if g == 0:
            total[...] = part
        else:
            total[...] += part


def finish(m, read, skip, total, wide, gate, mixed):
    read(m, 2, gate)
    read(m, 1, wide)
    lane = lax.broadcasted_iota(jnp.int32, (BLOCKS, LANES), 1)
    for a in range(TILES - 1):
        for f in range(SUBS):
            row = BLOCKS * (TILES * f + a + 1)
            first = total[row : row + BLOCKS, 0:LANES]
            second = total[row : row + BLOCKS, LANES : 2 * LANES]
            if f == 0:
                low, high = first, second
                continue
            before = pltpu.roll(total[row - BLOCKS : row, LANES : 2 * LANES], PART * f, 1)
            first, second = pltpu.roll(first, PART * f, 1), pltpu.roll(second, PART * f, 1)
            low = low + jnp.where(lane >= PART * f, first, before)
            high = high + jnp.where(lane >= PART * f, second, first)
        for b, y in ((2 * a, low), (2 * a + 1, high)):
            rows = pl.ds(b, BLOCKS, stride=SUBS)
            mixed[rows, :] = gate[rows, :] * (y + skip * wide[rows, :])


def kernel(
    x_hbm, g_hbm, h_hbm, w_hbm, far_hbm, skip_hbm, out,
    x_in, g_in, h_in, w_in, far_in, skip_in,
    stage, packed, got, far_mine, far_got, w_got,
    taps, wide, x_own, g_own, mixed, masks, turned, base0, edges0, total0, base1, edges1, total1,
    ready, back, regroup, sliced, part, result,
    w_wide, w_sorted, load_sem, own_sem, in_send, in_recv, g_send, g_recv, far_send, far_recv, w_send, w_recv,
    m_send, m_recv, t_send, t_recv, o_send, o_recv,
):
    me_c, me_h = lax.axis_index("ctx"), lax.axis_index("head")

    def remote(src, dst, send, recv, axis, k):
        me, n = (me_c, NC) if axis == "ctx" else (me_h, NH)
        return pltpu.make_async_remote_copy(
            src_ref=src, dst_ref=dst, send_sem=send, recv_sem=recv,
            device_id={axis: lax.rem(me + k, n)}, device_id_type=MESH,
        )

    def far_copy(k):
        return remote(far_mine, far_got.at[me_c], far_send.at[k], far_recv.at[k], "ctx", k)

    def w_copy(k):
        return remote(w_sorted, w_got.at[me_h], w_send.at[k], w_recv.at[k], "head", k)

    def in_copy(m, k):
        rows = pl.ds(pl.multiple_of(m * PER, 16), PER)
        peer = lax.rem(me_c + k, NC)
        return remote(
            packed.at[peer, rows], got.at[me_c, rows], in_send.at[m, k], in_recv.at[m, k], "ctx", k
        )

    def gate_copy(k):
        rows = pl.ds(GATES, MINE * ROWS)
        peer = lax.rem(me_c + k, NC)
        return remote(
            packed.at[peer, rows], got.at[me_c, rows], g_send.at[k], g_recv.at[k], "ctx", k
        )

    def m_copy(m, k):
        rows = pl.ds(pl.multiple_of(m * ROWS, 16), ROWS)
        peer = lax.rem(me_c + k, NC)
        return remote(
            ready.at[peer, rows], back.at[me_c, rows], m_send.at[m, k], m_recv.at[m, k], "ctx", k
        )

    def t_copy(t, k):
        peer = lax.rem(me_h + k, NH)
        return remote(
            sliced.at[t, peer], part.at[t, me_h], t_send.at[t, k], t_recv.at[t, k], "head", k
        )

    columns = pl.ds(pl.multiple_of(me_h * LANES, LANES), LANES)

    def o_copy(k):
        peer = lax.rem(me_h + k, NH)
        return remote(result.at[peer], out.at[:, columns], o_send.at[k], o_recv.at[k], "head", k)

    loads = [
        pltpu.make_async_copy(a, b, load_sem.at[i])
        for i, (a, b) in enumerate(
            (
                (h_hbm, h_in), (x_hbm, x_in), (g_hbm, g_in), (far_hbm, far_in),
                (skip_hbm, skip_in), (w_hbm, w_in),
            )
        )
    ]
    for copy in loads:
        copy.start()
    greet(me_c, me_h)

    def pack(a, ref):
        for s in range(ROWS):
            stage[a, pl.ds(s, CH, stride=ROWS), :] = ref[:, LANES * s : LANES * (s + 1)].astype(F32)
        for c in range(NC):
            for m in range(MINE):
                ch = MINE * c + m
                lo = PER * m + ROWS * a if a < 2 else GATES + ROWS * m
                packed[c, lo : lo + ROWS, :] = stage[a, ROWS * ch : ROWS * (ch + 1), :].astype(BF16)

    loads[0].wait()
    pack(0, h_in)
    loads[1].wait()
    pack(1, x_in)
    pl.semaphore_wait(pltpu.get_barrier_semaphore(), NC - 1 + NH - 1)
    for m in range(MINE):
        for k in range(1, NC):
            in_copy(m, k).start()
    for copy in loads[2:]:
        copy.wait()
    row = lax.broadcasted_iota(jnp.int32, (8, LANES), 0)
    table = jnp.full((8, LANES), -1, jnp.int32)
    for r in range(2):
        for k in range(4):
            table = jnp.where(row == 4 * r + k, far_in[r, k], table)
    far_mine[...] = table
    for k in range(1, NC):
        far_copy(k).start()
    pack(2, g_in)
    for k in range(1, NC):
        gate_copy(k).start()
    for j in range(4):
        w_wide[j] = w_in[:, LANES * j : LANES * (j + 1)].astype(F32)
        for m in range(0, MINE, 2):
            rows = [w_wide[j, pl.ds(m + i, NC, stride=MINE), :] for i in range(2)]
            w_sorted[NC * m : NC * (m + 2), LANES * j : LANES * (j + 1)] = jnp.concatenate(
                rows, axis=0
            ).astype(BF16)
    for k in range(1, NH):
        w_copy(k).start()
    own = [
        pltpu.make_async_copy(a, b, own_sem.at[i])
        for i, (a, b) in enumerate(
            (
                (far_mine, far_got.at[me_c]), (packed.at[me_c], got.at[me_c]), (w_sorted, w_got.at[me_h]),
            )
        )
    ]
    for copy in own:
        copy.start()
    for copy in own:
        copy.wait()
    empty = jnp.zeros((BLOCKS, LANES), F32)
    for f in range(SUBS):
        for a in range(TILES):
            base0[f, a, 0:BLOCKS, :] = empty
            base1[f, a, 0:BLOCKS, :] = empty
        for b in range(SUBS):
            turned[b, f, 0:BLOCKS, :] = empty
    edges0[0:PART, :] = empty.astype(BF16)
    edges1[0:PART, :] = empty.astype(BF16)
    for k in range(1, NC):
        far_copy(k).wait()
    for c in range(NC):
        regroup[8 * c : 8 * c + 8, :] = far_got[c]
    read_masks(regroup, masks)

    def read(m, a, to):
        lo = m * PER + a * ROWS if a < 2 else GATES + m * ROWS
        rows = pl.ds(pl.multiple_of(lo, 16), ROWS)
        for c in range(NC):
            to[ROWS * c : ROWS * (c + 1), :] = got[c, rows, :].astype(F32)

    def arrive(m):
        for k in range(1, NC):
            in_copy(m, k).wait()

    def hand_back(m, total):
        finish(m, read, skip_in[MINE * me_c + m], total, x_own, g_own, mixed)
        for c in range(NC):
            ready[c, pl.ds(pl.multiple_of(m * ROWS, 16), ROWS), :] = mixed[
                ROWS * c : ROWS * (c + 1), :
            ].astype(BF16)

    def send_back(m):
        for k in range(1, NC):
            m_copy(m, k).start()

    def pass_on(t):
        for m in (2 * t, 2 * t + 1):
            for k in range(1, NC):
                m_copy(m, k).wait()
        for c in range(NC):
            for i in range(2):
                stage[0, ROWS * (2 * c + i) : ROWS * (2 * c + i + 1), :] = jnp.where(
                    me_c == c,
                    ready[c, ROWS * (2 * t + i) : ROWS * (2 * t + i + 1), :].astype(F32),
                    back[c, ROWS * (2 * t + i) : ROWS * (2 * t + i + 1), :].astype(F32),
                )
        for h in range(NH):
            rows = [stage[0, pl.ds(ROWS * i + h, NC, stride=2 * ROWS), :] for i in range(2)]
            sliced[t, h] = jnp.concatenate(rows, axis=0).astype(BF16)
        for k in range(1, NH):
            t_copy(t, k).start()

    arrive(0)
    prepare(0, read, taps, wide, turned, base0, edges0)

    def pair(t, _):
        arrive(2 * t + 1)
        multiply(masks, base0, edges0, total0)
        prepare(2 * t + 1, read, taps, wide, turned, base1, edges1)

        @pl.when(t == 0)
        def _():
            arrive(2)
            for k in range(1, NC):
                gate_copy(k).wait()

        @pl.when(t == 1)
        def _():
            pass_on(0)

        multiply(masks, base1, edges1, total1)
        prepare(jnp.minimum(2 * t + 2, MINE - 1), read, taps, wide, turned, base0, edges0)
        hand_back(2 * t, total0)
        send_back(2 * t)
        hand_back(2 * t + 1, total1)
        send_back(2 * t + 1)
        return 0

    lax.fori_loop(0, MINE // 2, pair, 0)
    pass_on(1)
    for t in range(2):
        copy = pltpu.make_async_copy(sliced.at[t, me_h], part.at[t, me_h], own_sem.at[3 + t])
        copy.start()
        copy.wait()
    for k in range(1, NH):
        w_copy(k).wait()
    total = None
    for t in range(2):
        for k in range(1, NH):
            t_copy(t, k).wait()
        half = lax.dot_general(
            w_got[:, 16 * t : 16 * t + 16, :].reshape(NH * 16, NH * CH),
            part[t].reshape(NH * 16, LANES),
            (((0,), (0,)), ((), ())),
            preferred_element_type=F32,
        )
        total = half if t == 0 else total + half
    for t in range(NH):
        result[t] = total[CH * t : CH * (t + 1), :]
    for k in range(1, NH):
        o_copy(k).start()
    copy = pltpu.make_async_copy(result.at[me_h], out.at[:, columns], own_sem.at[5])
    copy.start()
    copy.wait()
    for k in range(1, NH):
        o_copy(k).wait()


def local(inputs, gate, filter_taps, skip, w_out, far_pairs):
    hbm = pl.BlockSpec(memory_space=pltpu.HBM)
    dma = pltpu.SemaphoreType.DMA
    vmem = pltpu.VMEM
    arrays = (inputs, gate, filter_taps, w_out, far_pairs, skip)
    return pl.pallas_call(
        kernel,
        out_shape=jax.ShapeDtypeStruct((CH, NH * LANES), F32),
        in_specs=[hbm] * 6,
        out_specs=hbm,
        scratch_shapes=[
            vmem(inputs.shape, BF16), vmem(gate.shape, BF16), vmem(filter_taps.shape, F32),
            vmem(w_out.shape, BF16), pltpu.SMEM(far_pairs.shape, jnp.int32), pltpu.SMEM(skip.shape, F32),
            vmem((3, CH * ROWS, LANES), F32),
            vmem((NC, GATES + MINE * ROWS, LANES), BF16),
            vmem((NC, GATES + MINE * ROWS, LANES), BF16),
            vmem((8, LANES), jnp.int32),
            vmem((NC, 8, LANES), jnp.int32),
            vmem((NH, CH, NH * CH), BF16),
            *[vmem((PIECES, LANES), F32)] * 5,
            vmem((TILES, BLOCKS, BLOCKS, LANES), F32),
            vmem((SUBS, SUBS, 2 * BLOCKS, LANES), F32),
            *[
                vmem((SUBS, TILES, 2 * BLOCKS, LANES), F32),
                vmem((PART * (PIECES + 1), LANES), BF16),
                vmem((SUBS * TILES * BLOCKS, 2 * LANES), F32),
            ]
            * 2,
            vmem((NC, MINE * ROWS, LANES), BF16),
            vmem((NC, MINE * ROWS, LANES), BF16),
            vmem((NC * 8, LANES), jnp.int32),
            vmem((2, NH, 16, LANES), BF16),
            vmem((2, NH, 16, LANES), BF16),
            vmem((NH, CH, LANES), F32),
            vmem((4, CH, LANES), F32),
            vmem((CH, NH * CH), BF16),
            dma((6,)), dma((6,)), dma((MINE, NC)), dma((MINE, NC)), dma((NC,)), dma((NC,)),
            dma((NC,)), dma((NC,)), dma((NH,)), dma((NH,)), dma((MINE, NC)), dma((MINE, NC)),
            dma((2, NH)), dma((2, NH)), dma((NH,)), dma((NH,)),
        ],
        compiler_params=pltpu.CompilerParams(
            collective_id=0, has_side_effects=True, vmem_limit_bytes=40 << 20
        ),
    )(*(pltpu.with_memory_space_constraint(a, pltpu.HBM) for a in arrays))


def solution(mesh):
    in_specs = (
        P("head", "ctx"),
        P("head", "ctx"),
        P("head", "ctx"),
        P("head"),
        P("head", None),
        P("ctx", None),
    )
    out_specs = P("head", "ctx")
    return jax.shard_map(local, mesh=mesh, in_specs=in_specs, out_specs=out_specs, check_vma=False)
```

```python
import jax
import jax.numpy as jnp
from jax import lax
from jax.experimental import pallas as pl
from jax.experimental.pallas import tpu as pltpu
from jax.sharding import PartitionSpec as P

F32 = jnp.float32
BF16 = jnp.bfloat16
LANES = 128
BLOCKS = 16
SUBS = 8
PIECES = BLOCKS * SUBS
NC = 8
NH = 16
CH = 32
MINE = CH // NC
ROWS = 16
PER = 2 * ROWS
TAPS = ROWS
GATES = TAPS + MINE * PER
LEGS = ((0, TAPS + PER), (TAPS + PER, (MINE - 1) * PER), (GATES, MINE * ROWS))
WIN = 2
PART = 16
TILES = 5
MESH = pl.DeviceIdType.MESH


def greet(me_c, me_h):
    barrier = pltpu.get_barrier_semaphore()
    for k in range(1, NC):
        pl.semaphore_signal(
            barrier, inc=1, device_id={"ctx": lax.rem(me_c + k, NC)}, device_id_type=MESH
        )
    for k in range(1, NH):
        pl.semaphore_signal(
            barrier, inc=1, device_id={"head": lax.rem(me_h + k, NH)}, device_id_type=MESH
        )


def read_masks(far, masks):
    block = lax.broadcasted_iota(jnp.int32, (BLOCKS, LANES), 0).astype(F32)
    chunk = lax.broadcasted_iota(jnp.int32, (BLOCKS, LANES), 1) // PART

    def reads(lag):
        if lag < WIN:
            return jnp.ones((BLOCKS, LANES), F32)
        mask = jnp.zeros((BLOCKS, LANES), F32)
        if lag < BLOCKS:
            for k in range(4):
                mask = jnp.where(far[pl.ds(k, BLOCKS, stride=4), :] == block - lag, 1.0, mask)
        return mask

    now = reads(0)
    for d in range(BLOCKS):
        after = reads(d + 1)
        masks[0, d] = after
        for a in range(1, TILES - 1):
            masks[a, d] = jnp.where(chunk <= 2 * a - 1, now, after)
        masks[TILES - 1, d] = now
        now = after


def prepare(m, read, taps, wide, turned, base, edges):
    read(m, 1, wide)
    read(m, 0, taps)
    lane = lax.broadcasted_iota(jnp.int32, (PART, LANES), 1)
    chunk = lane // PART
    for b in range(SUBS):
        piece = wide[pl.ds(b, BLOCKS, stride=SUBS), :]
        for s in range(SUBS):
            turned[b, s, BLOCKS : 2 * BLOCKS, :] = pltpu.roll(piece, PART * s, 1) if s else piece
    for f in range(SUBS):
        for a in range(TILES):
            tile = None
            for v in range(SUBS):
                b = 2 * a - 1 - v
                lo = BLOCKS if b >= 0 else BLOCKS - 1
                piece = turned[b % SUBS, (v - f) % SUBS, lo : lo + BLOCKS, :]
                tile = piece if tile is None else jnp.where(chunk == v, piece, tile)
            base[f, a, BLOCKS : 2 * BLOCKS, :] = tile
    keep = lane >= lax.broadcasted_iota(jnp.int32, (PART, LANES), 0)
    before = jnp.zeros((PART, LANES), F32)
    for p in range(PIECES):
        row = jnp.broadcast_to(taps[p : p + 1, :], (PART, LANES))
        turn = pltpu.roll(row, 0, 1, stride=1, stride_axis=0)
        edges[PART * (p + 1) : PART * (p + 2), :] = jnp.where(keep, turn, before).astype(BF16)
        before = turn


def multiply(masks, base, edges, total):
    for g in range(0, BLOCKS, 2):
        left = []
        for f in range(SUBS):
            for a in range(TILES):
                left.append(
                    jnp.concatenate(
                        [
                            (base[f, a, BLOCKS - d : 2 * BLOCKS - d, :] * masks[a, d]).astype(BF16)
                            for d in (g, g + 1)
                        ],
                        axis=1,
                    )
                )
        lo = LANES * g
        right = jnp.concatenate(
            [edges[lo : lo + 256, :], edges[lo + PART : lo + PART + 256, :]], axis=1
        )
        part = jnp.dot(jnp.concatenate(left, axis=0), right, preferred_element_type=F32)
        if g == 0:
            total[...] = part
        else:
            total[...] += part


def finish(m, read, skip, total, wide, gate, mixed):
    read(m, 2, gate)
    read(m, 1, wide)
    lane = lax.broadcasted_iota(jnp.int32, (BLOCKS, LANES), 1)
    for a in range(TILES - 1):
        for f in range(SUBS):
            row = BLOCKS * (TILES * f + a + 1)
            first = total[row : row + BLOCKS, 0:LANES]
            second = total[row : row + BLOCKS, LANES : 2 * LANES]
            if f == 0:
                low, high = first, second
                continue
            before = pltpu.roll(total[row - BLOCKS : row, LANES : 2 * LANES], PART * f, 1)
            first, second = pltpu.roll(first, PART * f, 1), pltpu.roll(second, PART * f, 1)
            low = low + jnp.where(lane >= PART * f, first, before)
            high = high + jnp.where(lane >= PART * f, second, first)
        for b, y in ((2 * a, low), (2 * a + 1, high)):
            rows = pl.ds(b, BLOCKS, stride=SUBS)
            mixed[rows, :] = gate[rows, :] * (y + skip * wide[rows, :])


def kernel(
    x_hbm, g_hbm, h_hbm, w_hbm, far_hbm, skip_hbm, out,
    x_in, g_in, h_in, w_in, far_in, skip_in,
    stage, packed, got, w_got,
    taps, wide, x_own, g_own, mixed, masks, turned, base0, edges0, total0, base1, edges1, total1,
    ready, back, regroup, sliced, part, result,
    load_sem, own_sem, in_send, in_recv, w_send, w_recv,
    m_send, m_recv, t_send, t_recv, o_send, o_recv,
):
    me_c, me_h = lax.axis_index("ctx"), lax.axis_index("head")

    def remote(src, dst, send, recv, axis, k):
        me, n = (me_c, NC) if axis == "ctx" else (me_h, NH)
        return pltpu.make_async_remote_copy(
            src_ref=src, dst_ref=dst, send_sem=send, recv_sem=recv,
            device_id={axis: lax.rem(me + k, n)}, device_id_type=MESH,
        )

    def w_copy(k):
        return remote(w_in, w_got.at[me_h], w_send.at[k], w_recv.at[k], "head", k)

    def in_copy(leg, k):
        rows = pl.ds(*LEGS[leg])
        peer = lax.rem(me_c + k, NC)
        return remote(
            packed.at[peer, rows], got.at[me_c, rows], in_send.at[leg, k], in_recv.at[leg, k], "ctx", k
        )

    def m_copy(t, k):
        rows = pl.ds(pl.multiple_of(t * 2 * ROWS, 16), 2 * ROWS)
        peer = lax.rem(me_c + k, NC)
        return remote(
            ready.at[peer, rows], back.at[me_c, rows], m_send.at[t, k], m_recv.at[t, k], "ctx", k
        )

    def t_copy(k):
        peer = lax.rem(me_h + k, NH)
        return remote(sliced.at[peer], part.at[me_h], t_send.at[k], t_recv.at[k], "head", k)

    columns = pl.ds(pl.multiple_of(me_h * LANES, LANES), LANES)

    def o_copy(k):
        peer = lax.rem(me_h + k, NH)
        return remote(result.at[peer], out.at[:, columns], o_send.at[k], o_recv.at[k], "head", k)

    greet(me_c, me_h)
    loads = [
        pltpu.make_async_copy(a, b, load_sem.at[i])
        for i, (a, b) in enumerate(
            (
                (h_hbm, h_in), (x_hbm, x_in), (far_hbm, far_in), (g_hbm, g_in),
                (skip_hbm, skip_in), (w_hbm, w_in),
            )
        )
    ]
    for copy in loads:
        copy.start()

    def spread(a, ref):
        for s in range(ROWS):
            stage[a, pl.ds(s, CH, stride=ROWS), :] = ref[:, LANES * s : LANES * (s + 1)].astype(F32)

    def pack(a, m):
        lo = TAPS + PER * m + ROWS * a if a < 2 else GATES + ROWS * m
        for c in range(NC):
            ch = MINE * c + m
            packed[c, lo : lo + ROWS, :] = stage[a, ROWS * ch : ROWS * (ch + 1), :].astype(BF16)

    def depart(leg):
        for k in range(1, NC):
            in_copy(leg, k).start()

    loads[2].wait()
    row = lax.broadcasted_iota(jnp.int32, (ROWS, LANES), 0)
    table = jnp.full((ROWS, LANES), -1, jnp.int32)
    for r in range(2):
        for k in range(4):
            table = jnp.where(row == 4 * r + k, far_in[r, k], table)
    table = table.astype(F32).astype(BF16)
    for c in range(NC):
        packed[c, 0:ROWS, :] = table
    for a in range(2):
        loads[a].wait()
        spread(a, (h_in, x_in)[a])
        pack(a, 0)
    pl.semaphore_wait(pltpu.get_barrier_semaphore(), NC - 1 + NH - 1)
    depart(0)
    for a in range(2):
        for m in range(1, MINE):
            pack(a, m)
    depart(1)
    for copy in loads[3:]:
        copy.wait()
    spread(2, g_in)
    for m in range(MINE):
        pack(2, m)
    depart(2)
    for k in range(1, NH):
        w_copy(k).start()
    own = [
        pltpu.make_async_copy(a, b, own_sem.at[i])
        for i, (a, b) in enumerate(
            (
                (packed.at[me_c], got.at[me_c]), (w_in, w_got.at[me_h]),
            )
        )
    ]
    for copy in own:
        copy.start()
    for copy in own:
        copy.wait()
    empty = jnp.zeros((BLOCKS, LANES), F32)
    for f in range(SUBS):
        for a in range(TILES):
            base0[f, a, 0:BLOCKS, :] = empty
            base1[f, a, 0:BLOCKS, :] = empty
        for b in range(SUBS):
            turned[b, f, 0:BLOCKS, :] = empty
    edges0[0:PART, :] = empty.astype(BF16)
    edges1[0:PART, :] = empty.astype(BF16)

    def arrive(leg):
        for k in range(1, NC):
            in_copy(leg, k).wait()

    arrive(0)
    for c in range(NC):
        regroup[8 * c : 8 * c + 8, :] = got[c, 0:ROWS, :].astype(F32)[0:8]
    read_masks(regroup, masks)

    def read(m, a, to):
        lo = TAPS + m * PER + a * ROWS if a < 2 else GATES + m * ROWS
        rows = pl.ds(pl.multiple_of(lo, 16), ROWS)
        for c in range(NC):
            to[ROWS * c : ROWS * (c + 1), :] = got[c, rows, :].astype(F32)

    def hand_back(m, total):
        finish(m, read, skip_in[MINE * me_c + m], total, x_own, g_own, mixed)
        for c in range(NC):
            ready[c, pl.ds(pl.multiple_of(m * ROWS, 16), ROWS), :] = mixed[
                ROWS * c : ROWS * (c + 1), :
            ].astype(BF16)

    def send_back(t):
        for k in range(1, NC):
            m_copy(t, k).start()

    prepare(0, read, taps, wide, turned, base0, edges0)

    def pair(t, _):
        @pl.when(t == 0)
        def _():
            arrive(1)

        multiply(masks, base0, edges0, total0)
        prepare(2 * t + 1, read, taps, wide, turned, base1, edges1)

        @pl.when(t == 0)
        def _():
            arrive(2)

        multiply(masks, base1, edges1, total1)
        prepare(jnp.minimum(2 * t + 2, MINE - 1), read, taps, wide, turned, base0, edges0)
        hand_back(2 * t, total0)
        hand_back(2 * t + 1, total1)
        send_back(t)
        return 0

    lax.fori_loop(0, MINE // 2, pair, 0)
    for t in range(2):
        for k in range(1, NC):
            m_copy(t, k).wait()
    for c in range(NC):
        stage[0, 64 * c : 64 * c + 64, :] = jnp.where(
            me_c == c, ready[c].astype(F32), back[c].astype(F32)
        )
    for t in range(NH):
        sliced[t] = stage[0, pl.ds(t, CH, stride=NH), :].astype(BF16)
    for k in range(1, NH):
        t_copy(k).start()
    copy = pltpu.make_async_copy(sliced.at[me_h], part.at[me_h], own_sem.at[3])
    copy.start()
    copy.wait()
    for k in range(1, NH):
        w_copy(k).wait()
    for k in range(1, NH):
        t_copy(k).wait()
    total = lax.dot_general(
        w_got[...].reshape(NH * CH, NH * CH), part[...].reshape(NH * CH, LANES),
        (((0,), (0,)), ((), ())), preferred_element_type=F32,
    )
    for t in range(NH):
        result[t] = total[CH * t : CH * (t + 1), :]
    for k in range(1, NH):
        o_copy(k).start()
    copy = pltpu.make_async_copy(result.at[me_h], out.at[:, columns], own_sem.at[5])
    copy.start()
    copy.wait()
    for k in range(1, NH):
        o_copy(k).wait()


def local(inputs, gate, filter_taps, skip, w_out, far_pairs):
    hbm = pl.BlockSpec(memory_space=pltpu.HBM)
    dma = pltpu.SemaphoreType.DMA
    vmem = pltpu.VMEM
    arrays = (inputs, gate, filter_taps, w_out, far_pairs, skip)
    return pl.pallas_call(
        kernel,
        out_shape=jax.ShapeDtypeStruct((CH, NH * LANES), F32),
        in_specs=[hbm] * 6,
        out_specs=hbm,
        scratch_shapes=[
            vmem(inputs.shape, BF16), vmem(gate.shape, BF16), vmem(filter_taps.shape, F32),
            vmem(w_out.shape, BF16), pltpu.SMEM(far_pairs.shape, jnp.int32), pltpu.SMEM(skip.shape, F32),
            vmem((3, CH * ROWS, LANES), F32),
            vmem((NC, GATES + MINE * ROWS, LANES), BF16),
            vmem((NC, GATES + MINE * ROWS, LANES), BF16),
            vmem((NH, CH, NH * CH), BF16),
            *[vmem((PIECES, LANES), F32)] * 5,
            vmem((TILES, BLOCKS, BLOCKS, LANES), F32),
            vmem((SUBS, SUBS, 2 * BLOCKS, LANES), F32),
            *[
                vmem((SUBS, TILES, 2 * BLOCKS, LANES), F32),
                vmem((PART * (PIECES + 1), LANES), BF16),
                vmem((SUBS * TILES * BLOCKS, 2 * LANES), F32),
            ]
            * 2,
            vmem((NC, MINE * ROWS, LANES), BF16),
            vmem((NC, MINE * ROWS, LANES), BF16),
            vmem((NC * 8, LANES), F32),
            vmem((NH, CH, LANES), BF16),
            vmem((NH, CH, LANES), BF16),
            vmem((NH, CH, LANES), F32),
            dma((6,)), dma((6,)), dma((3, NC)), dma((3, NC)), dma((NH,)), dma((NH,)),
            dma((2, NC)), dma((2, NC)), dma((NH,)), dma((NH,)), dma((NH,)), dma((NH,)),
        ],
        compiler_params=pltpu.CompilerParams(
            collective_id=0, has_side_effects=True, vmem_limit_bytes=40 << 20
        ),
    )(*(pltpu.with_memory_space_constraint(a, pltpu.HBM) for a in arrays))


def solution(mesh):
    in_specs = (
        P("head", "ctx"),
        P("head", "ctx"),
        P("head", "ctx"),
        P("head"),
        P("head", None),
        P("ctx", None),
    )
    out_specs = P("head", "ctx")
    return jax.shard_map(local, mesh=mesh, in_specs=in_specs, out_specs=out_specs, check_vma=False)
```

```python
import jax
import jax.numpy as jnp
from jax import lax
from jax.experimental import pallas as pl
from jax.experimental.pallas import tpu as pltpu
from jax.sharding import PartitionSpec as P

F32 = jnp.float32
BF16 = jnp.bfloat16
LANES = 128
BLOCKS = 16
SUBS = 8
PIECES = BLOCKS * SUBS
NC = 8
NH = 16
CH = 32
MINE = CH // NC
ROWS = 16
PER = 2 * ROWS
TAPS = ROWS
GATES = TAPS + MINE * PER
LEGS = ((0, TAPS + 2 * PER), (TAPS + 2 * PER, 2 * PER), (GATES, MINE * ROWS))
WIN = 2
PART = 16
TILES = 5
MESH = pl.DeviceIdType.MESH


def greet(me_c, me_h):
    barrier = pltpu.get_barrier_semaphore()
    for k in range(1, NC):
        pl.semaphore_signal(
            barrier, inc=1, device_id={"ctx": lax.rem(me_c + k, NC)}, device_id_type=MESH
        )
    for k in range(1, NH):
        pl.semaphore_signal(
            barrier, inc=1, device_id={"head": lax.rem(me_h + k, NH)}, device_id_type=MESH
        )


def read_masks(far, masks):
    block = lax.broadcasted_iota(jnp.int32, (BLOCKS, LANES), 0).astype(F32)
    chunk = lax.broadcasted_iota(jnp.int32, (BLOCKS, LANES), 1) // PART

    def reads(lag):
        if lag < WIN:
            return jnp.ones((BLOCKS, LANES), F32)
        mask = jnp.zeros((BLOCKS, LANES), F32)
        if lag < BLOCKS:
            for k in range(4):
                mask = jnp.where(far[pl.ds(k, BLOCKS, stride=4), :] == block - lag, 1.0, mask)
        return mask

    now = reads(0)
    for d in range(BLOCKS):
        after = reads(d + 1)
        masks[0, d] = after
        for a in range(1, TILES - 1):
            masks[a, d] = jnp.where(chunk <= 2 * a - 1, now, after)
        masks[TILES - 1, d] = now
        now = after


def prepare(m, read, taps, wide, turned, base, edges):
    read(m, 1, wide)
    read(m, 0, taps)
    lane = lax.broadcasted_iota(jnp.int32, (PART, LANES), 1)
    chunk = lane // PART
    for b in range(SUBS):
        piece = wide[pl.ds(b, BLOCKS, stride=SUBS), :]
        for s in range(SUBS):
            turned[b, s, BLOCKS : 2 * BLOCKS, :] = pltpu.roll(piece, PART * s, 1) if s else piece
    for f in range(SUBS):
        for a in range(TILES):
            tile = None
            for v in range(SUBS):
                b = 2 * a - 1 - v
                lo = BLOCKS if b >= 0 else BLOCKS - 1
                piece = turned[b % SUBS, (v - f) % SUBS, lo : lo + BLOCKS, :]
                tile = piece if tile is None else jnp.where(chunk == v, piece, tile)
            base[f, a, BLOCKS : 2 * BLOCKS, :] = tile
    keep = lane >= lax.broadcasted_iota(jnp.int32, (PART, LANES), 0)
    before = jnp.zeros((PART, LANES), F32)
    for p in range(PIECES):
        row = jnp.broadcast_to(taps[p : p + 1, :], (PART, LANES))
        turn = pltpu.roll(row, 0, 1, stride=1, stride_axis=0)
        edges[PART * (p + 1) : PART * (p + 2), :] = jnp.where(keep, turn, before).astype(BF16)
        before = turn


def multiply(masks, base, edges, total):
    for g in range(0, BLOCKS, 2):
        left = []
        for f in range(SUBS):
            for a in range(TILES):
                left.append(
                    jnp.concatenate(
                        [
                            (base[f, a, BLOCKS - d : 2 * BLOCKS - d, :] * masks[a, d]).astype(BF16)
                            for d in (g, g + 1)
                        ],
                        axis=1,
                    )
                )
        lo = LANES * g
        right = jnp.concatenate(
            [edges[lo : lo + 256, :], edges[lo + PART : lo + PART + 256, :]], axis=1
        )
        part = jnp.dot(jnp.concatenate(left, axis=0), right, preferred_element_type=F32)
        if g == 0:
            total[...] = part
        else:
            total[...] += part


def finish(m, read, skip, total, wide, gate, mixed):
    read(m, 2, gate)
    read(m, 1, wide)
    lane = lax.broadcasted_iota(jnp.int32, (BLOCKS, LANES), 1)
    for a in range(TILES - 1):
        for f in range(SUBS):
            row = BLOCKS * (TILES * f + a + 1)
            first = total[row : row + BLOCKS, 0:LANES]
            second = total[row : row + BLOCKS, LANES : 2 * LANES]
            if f == 0:
                low, high = first, second
                continue
            before = pltpu.roll(total[row - BLOCKS : row, LANES : 2 * LANES], PART * f, 1)
            first, second = pltpu.roll(first, PART * f, 1), pltpu.roll(second, PART * f, 1)
            low = low + jnp.where(lane >= PART * f, first, before)
            high = high + jnp.where(lane >= PART * f, second, first)
        for b, y in ((2 * a, low), (2 * a + 1, high)):
            rows = pl.ds(b, BLOCKS, stride=SUBS)
            mixed[rows, :] = gate[rows, :] * (y + skip * wide[rows, :])


def kernel(
    x_hbm, g_hbm, h_hbm, w_hbm, far_hbm, skip_hbm, out,
    x_in, g_in, h_in, w_in, far_in, skip_in,
    stage, packed, got, w_got,
    taps, wide, x_own, g_own, mixed, masks, turned, base0, edges0, total0, base1, edges1, total1,
    ready, back, regroup, sliced, part, result,
    load_sem, own_sem, in_send, in_recv, w_send, w_recv,
    m_send, m_recv, t_send, t_recv, o_send, o_recv,
):
    me_c, me_h = lax.axis_index("ctx"), lax.axis_index("head")

    def remote(src, dst, send, recv, axis, k):
        me, n = (me_c, NC) if axis == "ctx" else (me_h, NH)
        return pltpu.make_async_remote_copy(
            src_ref=src, dst_ref=dst, send_sem=send, recv_sem=recv,
            device_id={axis: lax.rem(me + k, n)}, device_id_type=MESH,
        )

    def w_copy(k):
        return remote(w_in, w_got.at[me_h], w_send.at[k], w_recv.at[k], "head", k)

    def in_copy(leg, k):
        rows = pl.ds(*LEGS[leg])
        peer = lax.rem(me_c + k, NC)
        return remote(
            packed.at[peer, rows], got.at[me_c, rows], in_send.at[leg, k], in_recv.at[leg, k], "ctx", k
        )

    def m_copy(t, k):
        rows = pl.ds(pl.multiple_of(t * 2 * ROWS, 16), 2 * ROWS)
        peer = lax.rem(me_c + k, NC)
        return remote(
            ready.at[peer, rows], back.at[me_c, rows], m_send.at[t, k], m_recv.at[t, k], "ctx", k
        )

    def t_copy(k):
        peer = lax.rem(me_h + k, NH)
        return remote(sliced.at[peer], part.at[me_h], t_send.at[k], t_recv.at[k], "head", k)

    columns = pl.ds(pl.multiple_of(me_h * LANES, LANES), LANES)

    def o_copy(k):
        peer = lax.rem(me_h + k, NH)
        return remote(result.at[peer], out.at[:, columns], o_send.at[k], o_recv.at[k], "head", k)

    greet(me_c, me_h)
    loads = [
        pltpu.make_async_copy(a, b, load_sem.at[i])
        for i, (a, b) in enumerate(
            (
                (h_hbm, h_in), (x_hbm, x_in), (far_hbm, far_in), (g_hbm, g_in),
                (skip_hbm, skip_in), (w_hbm, w_in),
            )
        )
    ]
    for copy in loads:
        copy.start()

    def spread(a, ref):
        for s in range(ROWS):
            stage[a, pl.ds(s, CH, stride=ROWS), :] = ref[:, LANES * s : LANES * (s + 1)].astype(F32)

    def pack(a, m):
        lo = TAPS + PER * m + ROWS * a if a < 2 else GATES + ROWS * m
        for c in range(NC):
            ch = MINE * c + m
            packed[c, lo : lo + ROWS, :] = stage[a, ROWS * ch : ROWS * (ch + 1), :].astype(BF16)

    def depart(leg):
        for k in range(1, NC):
            in_copy(leg, k).start()

    loads[2].wait()
    row = lax.broadcasted_iota(jnp.int32, (ROWS, LANES), 0)
    table = jnp.full((ROWS, LANES), -1, jnp.int32)
    for r in range(2):
        for k in range(4):
            table = jnp.where(row == 4 * r + k, far_in[r, k], table)
    table = table.astype(F32).astype(BF16)
    for c in range(NC):
        packed[c, 0:ROWS, :] = table
    for a in range(2):
        loads[a].wait()
        spread(a, (h_in, x_in)[a])
        pack(a, 0)
        pack(a, 1)
    pl.semaphore_wait(pltpu.get_barrier_semaphore(), NC - 1 + NH - 1)
    depart(0)
    for a in range(2):
        for m in range(2, MINE):
            pack(a, m)
    depart(1)
    for copy in loads[3:]:
        copy.wait()
    spread(2, g_in)
    for m in range(MINE):
        pack(2, m)
    depart(2)
    for k in range(1, NH):
        w_copy(k).start()
    own = [
        pltpu.make_async_copy(a, b, own_sem.at[i])
        for i, (a, b) in enumerate(
            (
                (packed.at[me_c], got.at[me_c]), (w_in, w_got.at[me_h]),
            )
        )
    ]
    for copy in own:
        copy.start()
    for copy in own:
        copy.wait()
    empty = jnp.zeros((BLOCKS, LANES), F32)
    for f in range(SUBS):
        for a in range(TILES):
            base0[f, a, 0:BLOCKS, :] = empty
            base1[f, a, 0:BLOCKS, :] = empty
        for b in range(SUBS):
            turned[b, f, 0:BLOCKS, :] = empty
    edges0[0:PART, :] = empty.astype(BF16)
    edges1[0:PART, :] = empty.astype(BF16)

    def arrive(leg):
        for k in range(1, NC):
            in_copy(leg, k).wait()

    arrive(0)
    for c in range(NC):
        regroup[8 * c : 8 * c + 8, :] = got[c, 0:ROWS, :].astype(F32)[0:8]
    read_masks(regroup, masks)

    def read(m, a, to):
        lo = TAPS + m * PER + a * ROWS if a < 2 else GATES + m * ROWS
        rows = pl.ds(pl.multiple_of(lo, 16), ROWS)
        for c in range(NC):
            to[ROWS * c : ROWS * (c + 1), :] = got[c, rows, :].astype(F32)

    def hand_back(m, total):
        finish(m, read, skip_in[MINE * me_c + m], total, x_own, g_own, mixed)
        for c in range(NC):
            ready[c, pl.ds(pl.multiple_of(m * ROWS, 16), ROWS), :] = mixed[
                ROWS * c : ROWS * (c + 1), :
            ].astype(BF16)

    def send_back(t):
        for k in range(1, NC):
            m_copy(t, k).start()

    prepare(0, read, taps, wide, turned, base0, edges0)

    multiply(masks, base0, edges0, total0)
    prepare(1, read, taps, wide, turned, base1, edges1)
    arrive(1)
    arrive(2)
    multiply(masks, base1, edges1, total1)
    prepare(2, read, taps, wide, turned, base0, edges0)
    hand_back(0, total0)
    multiply(masks, base0, edges0, total0)
    prepare(3, read, taps, wide, turned, base1, edges1)
    hand_back(1, total1)
    send_back(0)
    multiply(masks, base1, edges1, total1)
    hand_back(2, total0)
    hand_back(3, total1)
    send_back(1)
    for t in range(2):
        for k in range(1, NC):
            m_copy(t, k).wait()
    for c in range(NC):
        stage[0, 64 * c : 64 * c + 64, :] = jnp.where(
            me_c == c, ready[c].astype(F32), back[c].astype(F32)
        )
    for t in range(NH):
        sliced[t] = stage[0, pl.ds(t, CH, stride=NH), :].astype(BF16)
    for k in range(1, NH):
        t_copy(k).start()
    copy = pltpu.make_async_copy(sliced.at[me_h], part.at[me_h], own_sem.at[3])
    copy.start()
    copy.wait()
    for k in range(1, NH):
        w_copy(k).wait()
    for k in range(1, NH):
        t_copy(k).wait()
    total = lax.dot_general(
        w_got[...].reshape(NH * CH, NH * CH), part[...].reshape(NH * CH, LANES),
        (((0,), (0,)), ((), ())), preferred_element_type=F32,
    )
    for t in range(NH):
        result[t] = total[CH * t : CH * (t + 1), :]
    for k in range(1, NH):
        o_copy(k).start()
    copy = pltpu.make_async_copy(result.at[me_h], out.at[:, columns], own_sem.at[5])
    copy.start()
    copy.wait()
    for k in range(1, NH):
        o_copy(k).wait()


def local(inputs, gate, filter_taps, skip, w_out, far_pairs):
    hbm = pl.BlockSpec(memory_space=pltpu.HBM)
    dma = pltpu.SemaphoreType.DMA
    vmem = pltpu.VMEM
    arrays = (inputs, gate, filter_taps, w_out, far_pairs, skip)
    return pl.pallas_call(
        kernel,
        out_shape=jax.ShapeDtypeStruct((CH, NH * LANES), F32),
        in_specs=[hbm] * 6,
        out_specs=hbm,
        scratch_shapes=[
            vmem(inputs.shape, BF16), vmem(gate.shape, BF16), vmem(filter_taps.shape, F32),
            vmem(w_out.shape, BF16), pltpu.SMEM(far_pairs.shape, jnp.int32), pltpu.SMEM(skip.shape, F32),
            vmem((3, CH * ROWS, LANES), F32),
            vmem((NC, GATES + MINE * ROWS, LANES), BF16),
            vmem((NC, GATES + MINE * ROWS, LANES), BF16),
            vmem((NH, CH, NH * CH), BF16),
            *[vmem((PIECES, LANES), F32)] * 5,
            vmem((TILES, BLOCKS, BLOCKS, LANES), F32),
            vmem((SUBS, SUBS, 2 * BLOCKS, LANES), F32),
            *[
                vmem((SUBS, TILES, 2 * BLOCKS, LANES), F32),
                vmem((PART * (PIECES + 1), LANES), BF16),
                vmem((SUBS * TILES * BLOCKS, 2 * LANES), F32),
            ]
            * 2,
            vmem((NC, MINE * ROWS, LANES), BF16),
            vmem((NC, MINE * ROWS, LANES), BF16),
            vmem((NC * 8, LANES), F32),
            vmem((NH, CH, LANES), BF16),
            vmem((NH, CH, LANES), BF16),
            vmem((NH, CH, LANES), F32),
            dma((6,)), dma((6,)), dma((3, NC)), dma((3, NC)), dma((NH,)), dma((NH,)),
            dma((2, NC)), dma((2, NC)), dma((NH,)), dma((NH,)), dma((NH,)), dma((NH,)),
        ],
        compiler_params=pltpu.CompilerParams(
            collective_id=0, has_side_effects=True, vmem_limit_bytes=40 << 20
        ),
    )(*(pltpu.with_memory_space_constraint(a, pltpu.HBM) for a in arrays))


def solution(mesh):
    in_specs = (
        P("head", "ctx"),
        P("head", "ctx"),
        P("head", "ctx"),
        P("head"),
        P("head", None),
        P("ctx", None),
    )
    out_specs = P("head", "ctx")
    return jax.shard_map(local, mesh=mesh, in_specs=in_specs, out_specs=out_specs, check_vma=False)
```

```python
import jax
import jax.numpy as jnp
from jax import lax
from jax.experimental import pallas as pl
from jax.experimental.pallas import tpu as pltpu
from jax.sharding import PartitionSpec as P

F32 = jnp.float32
BF16 = jnp.bfloat16
LANES = 128
BLOCKS = 16
SUBS = 8
PIECES = BLOCKS * SUBS
NC = 8
NH = 16
CH = 32
MINE = CH // NC
ROWS = 16
PER = 2 * ROWS
TAPS = ROWS
GATES = TAPS + MINE * PER
LEGS = ((0, TAPS + 2 * PER), (TAPS + 2 * PER, 2 * PER), (GATES, MINE * ROWS))
WIN = 2
PART = 16
TILES = 5
MESH = pl.DeviceIdType.MESH


def greet(me_c, me_h):
    barrier = pltpu.get_barrier_semaphore()
    for k in range(1, NC):
        pl.semaphore_signal(
            barrier, inc=1, device_id={"ctx": lax.rem(me_c + k, NC)}, device_id_type=MESH
        )
    for k in range(1, NH):
        pl.semaphore_signal(
            barrier, inc=1, device_id={"head": lax.rem(me_h + k, NH)}, device_id_type=MESH
        )


def read_masks(far, masks):
    block = lax.broadcasted_iota(jnp.int32, (BLOCKS, LANES), 0).astype(F32)
    chunk = lax.broadcasted_iota(jnp.int32, (BLOCKS, LANES), 1) // PART

    def reads(lag):
        if lag < WIN:
            return jnp.ones((BLOCKS, LANES), F32)
        mask = jnp.zeros((BLOCKS, LANES), F32)
        if lag < BLOCKS:
            for k in range(4):
                mask = jnp.where(far[pl.ds(k, BLOCKS, stride=4), :] == block - lag, 1.0, mask)
        return mask

    now = reads(0)
    for d in range(BLOCKS):
        after = reads(d + 1)
        masks[0, d] = after
        for a in range(1, TILES - 1):
            masks[a, d] = jnp.where(chunk <= 2 * a - 1, now, after)
        masks[TILES - 1, d] = now
        now = after


def prepare(m, read, taps, wide, turned, base, edges):
    read(m, 1, wide)
    read(m, 0, taps)
    lane = lax.broadcasted_iota(jnp.int32, (PART, LANES), 1)
    chunk = lane // PART
    for b in range(SUBS):
        piece = wide[pl.ds(b, BLOCKS, stride=SUBS), :]
        for s in range(SUBS):
            turned[b, s, BLOCKS : 2 * BLOCKS, :] = pltpu.roll(piece, PART * s, 1) if s else piece
    for f in range(SUBS):
        for a in range(TILES):
            if f == 0 and a == 0:
                continue
            tile = None
            for v in range(SUBS):
                b = 2 * a - 1 - v
                lo = BLOCKS if b >= 0 else BLOCKS - 1
                piece = turned[b % SUBS, (v - f) % SUBS, lo : lo + BLOCKS, :]
                tile = piece if tile is None else jnp.where(chunk == v, piece, tile)
            base[f, a, BLOCKS : 2 * BLOCKS, :] = tile
    keep = lane >= lax.broadcasted_iota(jnp.int32, (PART, LANES), 0)
    before = jnp.zeros((PART, LANES), F32)
    for p in range(PIECES):
        row = jnp.broadcast_to(taps[p : p + 1, :], (PART, LANES))
        turn = pltpu.roll(row, 0, 1, stride=1, stride_axis=0)
        edges[PART * (p + 1) : PART * (p + 2), :] = jnp.where(keep, turn, before).astype(BF16)
        before = turn


def multiply(masks, base, edges, total):
    for g in range(0, BLOCKS, 2):
        left = []
        for f in range(SUBS):
            for a in range(TILES):
                if f == 0 and a == 0:
                    continue
                left.append(
                    jnp.concatenate(
                        [
                            (base[f, a, BLOCKS - d : 2 * BLOCKS - d, :] * masks[a, d]).astype(BF16)
                            for d in (g, g + 1)
                        ],
                        axis=1,
                    )
                )
        lo = LANES * g
        right = jnp.concatenate(
            [edges[lo : lo + 256, :], edges[lo + PART : lo + PART + 256, :]], axis=1
        )
        part = jnp.dot(jnp.concatenate(left, axis=0), right, preferred_element_type=F32)
        if g == 0:
            total[...] = part
        else:
            total[...] += part


def finish(m, read, skip, total, wide, gate, mixed):
    read(m, 2, gate)
    read(m, 1, wide)
    lane = lax.broadcasted_iota(jnp.int32, (BLOCKS, LANES), 1)
    for a in range(TILES - 1):
        for f in range(SUBS):
            row = BLOCKS * (TILES * f + a)
            first = total[row : row + BLOCKS, 0:LANES]
            second = total[row : row + BLOCKS, LANES : 2 * LANES]
            if f == 0:
                low, high = first, second
                continue
            before = pltpu.roll(total[row - BLOCKS : row, LANES : 2 * LANES], PART * f, 1)
            first, second = pltpu.roll(first, PART * f, 1), pltpu.roll(second, PART * f, 1)
            low = low + jnp.where(lane >= PART * f, first, before)
            high = high + jnp.where(lane >= PART * f, second, first)
        for b, y in ((2 * a, low), (2 * a + 1, high)):
            rows = pl.ds(b, BLOCKS, stride=SUBS)
            mixed[rows, :] = gate[rows, :] * (y + skip * wide[rows, :])


def kernel(
    x_hbm, g_hbm, h_hbm, w_hbm, far_hbm, skip_hbm, out,
    x_in, g_in, h_in, w_in, far_in, skip_in,
    stage, packed, got, w_got,
    taps, wide, x_own, g_own, mixed, masks, turned, base0, edges0, total0, base1, edges1, total1,
    ready, back, regroup, sliced, part, result,
    w_wide, w_sorted, load_sem, own_sem, in_send, in_recv, w_send, w_recv,
    m_send, m_recv, t_send, t_recv, o_send, o_recv,
):
    me_c, me_h = lax.axis_index("ctx"), lax.axis_index("head")

    def remote(src, dst, send, recv, axis, k):
        me, n = (me_c, NC) if axis == "ctx" else (me_h, NH)
        return pltpu.make_async_remote_copy(
            src_ref=src, dst_ref=dst, send_sem=send, recv_sem=recv,
            device_id={axis: lax.rem(me + k, n)}, device_id_type=MESH,
        )

    def w_copy(k):
        return remote(w_sorted, w_got.at[me_h], w_send.at[k], w_recv.at[k], "head", k)

    def in_copy(leg, k):
        rows = pl.ds(*LEGS[leg])
        peer = lax.rem(me_c + k, NC)
        return remote(
            packed.at[peer, rows], got.at[me_c, rows], in_send.at[leg, k], in_recv.at[leg, k], "ctx", k
        )

    def m_copy(t, k):
        rows = pl.ds(pl.multiple_of(t * 2 * ROWS, 16), 2 * ROWS)
        peer = lax.rem(me_c + k, NC)
        return remote(
            ready.at[peer, rows], back.at[me_c, rows], m_send.at[t, k], m_recv.at[t, k], "ctx", k
        )

    def t_copy(t, k):
        peer = lax.rem(me_h + k, NH)
        return remote(
            sliced.at[t, peer], part.at[t, me_h], t_send.at[t, k], t_recv.at[t, k], "head", k
        )

    columns = pl.ds(pl.multiple_of(me_h * LANES, LANES), LANES)

    def o_copy(k):
        peer = lax.rem(me_h + k, NH)
        return remote(result.at[peer], out.at[:, columns], o_send.at[k], o_recv.at[k], "head", k)

    greet(me_c, me_h)
    loads = [
        pltpu.make_async_copy(a, b, load_sem.at[i])
        for i, (a, b) in enumerate(
            (
                (h_hbm, h_in), (x_hbm, x_in), (far_hbm, far_in), (g_hbm, g_in),
                (skip_hbm, skip_in), (w_hbm, w_in),
            )
        )
    ]
    for copy in loads:
        copy.start()

    def spread(a, ref):
        for s in range(ROWS):
            stage[a, pl.ds(s, CH, stride=ROWS), :] = ref[:, LANES * s : LANES * (s + 1)].astype(F32)

    def pack(a, m):
        lo = TAPS + PER * m + ROWS * a if a < 2 else GATES + ROWS * m
        for c in range(NC):
            ch = MINE * c + m
            packed[c, lo : lo + ROWS, :] = stage[a, ROWS * ch : ROWS * (ch + 1), :].astype(BF16)

    def depart(leg):
        for k in range(1, NC):
            in_copy(leg, k).start()

    loads[2].wait()
    row = lax.broadcasted_iota(jnp.int32, (ROWS, LANES), 0)
    table = jnp.full((ROWS, LANES), -1, jnp.int32)
    for r in range(2):
        for k in range(4):
            table = jnp.where(row == 4 * r + k, far_in[r, k], table)
    table = table.astype(F32).astype(BF16)
    for c in range(NC):
        packed[c, 0:ROWS, :] = table
    for a in range(2):
        loads[a].wait()
        spread(a, (h_in, x_in)[a])
        pack(a, 0)
        pack(a, 1)
    pl.semaphore_wait(pltpu.get_barrier_semaphore(), NC - 1 + NH - 1)
    depart(0)
    for a in range(2):
        for m in range(2, MINE):
            pack(a, m)
    depart(1)
    for copy in loads[3:]:
        copy.wait()
    spread(2, g_in)
    for m in range(MINE):
        pack(2, m)
    depart(2)
    for j in range(4):
        w_wide[j] = w_in[:, LANES * j : LANES * (j + 1)].astype(F32)
        for m in range(0, MINE, 2):
            rows = [w_wide[j, pl.ds(m + i, NC, stride=MINE), :] for i in range(2)]
            w_sorted[NC * m : NC * (m + 2), LANES * j : LANES * (j + 1)] = jnp.concatenate(
                rows, axis=0
            ).astype(BF16)
    for k in range(1, NH):
        w_copy(k).start()
    own = [
        pltpu.make_async_copy(a, b, own_sem.at[i])
        for i, (a, b) in enumerate(
            (
                (packed.at[me_c], got.at[me_c]), (w_sorted, w_got.at[me_h]),
            )
        )
    ]
    for copy in own:
        copy.start()
    for copy in own:
        copy.wait()
    empty = jnp.zeros((BLOCKS, LANES), F32)
    for f in range(SUBS):
        for a in range(TILES):
            base0[f, a, 0:BLOCKS, :] = empty
            base1[f, a, 0:BLOCKS, :] = empty
        for b in range(SUBS):
            turned[b, f, 0:BLOCKS, :] = empty
    edges0[0:PART, :] = empty.astype(BF16)
    edges1[0:PART, :] = empty.astype(BF16)

    def arrive(leg):
        for k in range(1, NC):
            in_copy(leg, k).wait()

    arrive(0)
    for c in range(NC):
        regroup[8 * c : 8 * c + 8, :] = got[c, 0:ROWS, :].astype(F32)[0:8]
    read_masks(regroup, masks)

    def read(m, a, to):
        lo = TAPS + m * PER + a * ROWS if a < 2 else GATES + m * ROWS
        rows = pl.ds(pl.multiple_of(lo, 16), ROWS)
        for c in range(NC):
            to[ROWS * c : ROWS * (c + 1), :] = got[c, rows, :].astype(F32)

    def hand_back(m, total):
        finish(m, read, skip_in[MINE * me_c + m], total, x_own, g_own, mixed)
        for c in range(NC):
            ready[c, pl.ds(pl.multiple_of(m * ROWS, 16), ROWS), :] = mixed[
                ROWS * c : ROWS * (c + 1), :
            ].astype(BF16)

    def send_back(t):
        for k in range(1, NC):
            m_copy(t, k).start()

    prepare(0, read, taps, wide, turned, base0, edges0)

    multiply(masks, base0, edges0, total0)
    prepare(1, read, taps, wide, turned, base1, edges1)
    arrive(1)
    arrive(2)
    multiply(masks, base1, edges1, total1)
    prepare(2, read, taps, wide, turned, base0, edges0)
    hand_back(0, total0)
    multiply(masks, base0, edges0, total0)
    prepare(3, read, taps, wide, turned, base1, edges1)
    hand_back(1, total1)
    send_back(0)
    multiply(masks, base1, edges1, total1)
    hand_back(2, total0)
    hand_back(3, total1)
    send_back(1)
    for t in range(2):
        for k in range(1, NC):
            m_copy(t, k).wait()
        for c in range(NC):
            rows = slice(2 * ROWS * t, 2 * ROWS * (t + 1))
            stage[t, 2 * ROWS * c : 2 * ROWS * (c + 1), :] = jnp.where(
                me_c == c, ready[c, rows, :].astype(F32), back[c, rows, :].astype(F32)
            )
        for h in range(NH):
            rows = [stage[t, pl.ds(ROWS * i + h, NC, stride=2 * ROWS), :] for i in range(2)]
            sliced[t, h] = jnp.concatenate(rows, axis=0).astype(BF16)
        for k in range(1, NH):
            t_copy(t, k).start()
    own = [
        pltpu.make_async_copy(sliced.at[t, me_h], part.at[t, me_h], own_sem.at[3 + t])
        for t in range(2)
    ]
    for copy in own:
        copy.start()
    for copy in own:
        copy.wait()
    for k in range(1, NH):
        w_copy(k).wait()
    total = None
    for t in range(2):
        for k in range(1, NH):
            t_copy(t, k).wait()
        half = lax.dot_general(
            w_got[:, 16 * t : 16 * t + 16, :].reshape(NH * 16, NH * CH),
            part[t].reshape(NH * 16, LANES),
            (((0,), (0,)), ((), ())),
            preferred_element_type=F32,
        )
        total = half if t == 0 else total + half
    for t in range(NH):
        result[t] = total[CH * t : CH * (t + 1), :]
    for k in range(1, NH):
        o_copy(k).start()
    copy = pltpu.make_async_copy(result.at[me_h], out.at[:, columns], own_sem.at[5])
    copy.start()
    copy.wait()
    for k in range(1, NH):
        o_copy(k).wait()


def local(inputs, gate, filter_taps, skip, w_out, far_pairs):
    hbm = pl.BlockSpec(memory_space=pltpu.HBM)
    dma = pltpu.SemaphoreType.DMA
    vmem = pltpu.VMEM
    arrays = (inputs, gate, filter_taps, w_out, far_pairs, skip)
    return pl.pallas_call(
        kernel,
        out_shape=jax.ShapeDtypeStruct((CH, NH * LANES), F32),
        in_specs=[hbm] * 6,
        out_specs=hbm,
        scratch_shapes=[
            vmem(inputs.shape, BF16), vmem(gate.shape, BF16), vmem(filter_taps.shape, F32),
            vmem(w_out.shape, BF16), pltpu.SMEM(far_pairs.shape, jnp.int32), pltpu.SMEM(skip.shape, F32),
            vmem((3, CH * ROWS, LANES), F32),
            vmem((NC, GATES + MINE * ROWS, LANES), BF16),
            vmem((NC, GATES + MINE * ROWS, LANES), BF16),
            vmem((NH, CH, NH * CH), BF16),
            *[vmem((PIECES, LANES), F32)] * 5,
            vmem((TILES, BLOCKS, BLOCKS, LANES), F32),
            vmem((SUBS, SUBS, 2 * BLOCKS, LANES), F32),
            *[
                vmem((SUBS, TILES, 2 * BLOCKS, LANES), F32),
                vmem((PART * (PIECES + 1), LANES), BF16),
                vmem(((SUBS * TILES - 1) * BLOCKS, 2 * LANES), F32),
            ]
            * 2,
            vmem((NC, MINE * ROWS, LANES), BF16),
            vmem((NC, MINE * ROWS, LANES), BF16),
            vmem((NC * 8, LANES), F32),
            vmem((2, NH, 16, LANES), BF16),
            vmem((2, NH, 16, LANES), BF16),
            vmem((NH, CH, LANES), F32),
            vmem((4, CH, LANES), F32),
            vmem((CH, NH * CH), BF16),
            dma((6,)), dma((6,)), dma((3, NC)), dma((3, NC)), dma((NH,)), dma((NH,)),
            dma((2, NC)), dma((2, NC)), dma((2, NH)), dma((2, NH)), dma((NH,)), dma((NH,)),
        ],
        compiler_params=pltpu.CompilerParams(
            collective_id=0, has_side_effects=True, vmem_limit_bytes=40 << 20
        ),
    )(*(pltpu.with_memory_space_constraint(a, pltpu.HBM) for a in arrays))


def solution(mesh):
    in_specs = (
        P("head", "ctx"),
        P("head", "ctx"),
        P("head", "ctx"),
        P("head"),
        P("head", None),
        P("ctx", None),
    )
    out_specs = P("head", "ctx")
    return jax.shard_map(local, mesh=mesh, in_specs=in_specs, out_specs=out_specs, check_vma=False)
```

```python
import jax
import jax.numpy as jnp
from jax import lax
from jax.experimental import pallas as pl
from jax.experimental.pallas import tpu as pltpu
from jax.sharding import PartitionSpec as P

F32 = jnp.float32
BF16 = jnp.bfloat16
LANES = 128
BLOCKS = 16
SUBS = 8
PIECES = BLOCKS * SUBS
NC = 8
NH = 16
CH = 32
MINE = CH // NC
ROWS = 16
PER = 2 * ROWS
TAPS = ROWS
GATES = TAPS + MINE * PER
LEGS = ((0, TAPS + 2 * PER), (TAPS + 2 * PER, 2 * PER), (GATES, MINE * ROWS))
WIN = 2
PART = 16
TILES = 5
MESH = pl.DeviceIdType.MESH


def greet(me_c, me_h):
    barrier = pltpu.get_barrier_semaphore()
    for k in range(1, NC):
        pl.semaphore_signal(
            barrier, inc=1, device_id={"ctx": lax.rem(me_c + k, NC)}, device_id_type=MESH
        )
    for k in range(1, NH):
        pl.semaphore_signal(
            barrier, inc=1, device_id={"head": lax.rem(me_h + k, NH)}, device_id_type=MESH
        )


def read_masks(far, masks):
    block = lax.broadcasted_iota(jnp.int32, (BLOCKS, LANES), 0).astype(F32)
    chunk = lax.broadcasted_iota(jnp.int32, (BLOCKS, LANES), 1) // PART

    def reads(lag):
        if lag < WIN:
            return jnp.ones((BLOCKS, LANES), F32)
        mask = jnp.zeros((BLOCKS, LANES), F32)
        if lag < BLOCKS:
            for k in range(4):
                mask = jnp.where(far[pl.ds(k, BLOCKS, stride=4), :] == block - lag, 1.0, mask)
        return mask

    now = reads(0)
    for d in range(BLOCKS):
        after = reads(d + 1)
        masks[0, d] = after
        for a in range(1, TILES - 1):
            masks[a, d] = jnp.where(chunk <= 2 * a - 1, now, after)
        masks[TILES - 1, d] = now
        now = after


def prepare(m, read, taps, wide, turned, base, edges):
    read(m, 1, wide)
    read(m, 0, taps)
    lane = lax.broadcasted_iota(jnp.int32, (PART, LANES), 1)
    chunk = lane // PART
    for b in range(SUBS):
        piece = wide[pl.ds(b, BLOCKS, stride=SUBS), :]
        for s in range(SUBS):
            turned[b, s, BLOCKS : 2 * BLOCKS, :] = pltpu.roll(piece, PART * s, 1) if s else piece
    for f in range(SUBS):
        for a in range(TILES):
            if f == 0 and a == 0:
                continue
            tile = None
            for v in range(SUBS):
                b = 2 * a - 1 - v
                lo = BLOCKS if b >= 0 else BLOCKS - 1
                piece = turned[b % SUBS, (v - f) % SUBS, lo : lo + BLOCKS, :]
                tile = piece if tile is None else jnp.where(chunk == v, piece, tile)
            base[f, a, BLOCKS : 2 * BLOCKS, :] = tile
    keep = lane >= lax.broadcasted_iota(jnp.int32, (PART, LANES), 0)
    before = jnp.zeros((PART, LANES), F32)
    for p in range(PIECES):
        row = jnp.broadcast_to(taps[p : p + 1, :], (PART, LANES))
        turn = pltpu.roll(row, 0, 1, stride=1, stride_axis=0)
        edges[PART * (p + 1) : PART * (p + 2), :] = jnp.where(keep, turn, before).astype(BF16)
        before = turn


def multiply(masks, base, edges, total):
    for g in range(0, BLOCKS, 2):
        left = []
        for f in range(SUBS):
            for a in range(TILES):
                if f == 0 and a == 0:
                    continue
                left.append(
                    jnp.concatenate(
                        [
                            (base[f, a, BLOCKS - d : 2 * BLOCKS - d, :] * masks[a, d]).astype(BF16)
                            for d in (g, g + 1)
                        ],
                        axis=1,
                    )
                )
        lo = LANES * g
        right = jnp.concatenate(
            [edges[lo : lo + 256, :], edges[lo + PART : lo + PART + 256, :]], axis=1
        )
        part = jnp.dot(jnp.concatenate(left, axis=0), right, preferred_element_type=F32)
        if g == 0:
            total[...] = part
        else:
            total[...] += part


def finish(m, read, skip, total, wide, gate, mixed):
    read(m, 2, gate)
    read(m, 1, wide)
    lane = lax.broadcasted_iota(jnp.int32, (BLOCKS, LANES), 1)
    for a in range(TILES - 1):
        for f in range(SUBS):
            row = BLOCKS * (TILES * f + a)
            first = total[row : row + BLOCKS, 0:LANES]
            second = total[row : row + BLOCKS, LANES : 2 * LANES]
            if f == 0:
                low, high = first, second
                continue
            before = pltpu.roll(total[row - BLOCKS : row, LANES : 2 * LANES], PART * f, 1)
            first, second = pltpu.roll(first, PART * f, 1), pltpu.roll(second, PART * f, 1)
            low = low + jnp.where(lane >= PART * f, first, before)
            high = high + jnp.where(lane >= PART * f, second, first)
        for b, y in ((2 * a, low), (2 * a + 1, high)):
            rows = pl.ds(b, BLOCKS, stride=SUBS)
            mixed[rows, :] = gate[rows, :] * (y + skip * wide[rows, :])


def kernel(
    x_hbm, g_hbm, h_hbm, w_hbm, far_hbm, skip_hbm, out,
    x_in, g_in, h_in, w_in, far_in, skip_in,
    stage, packed, got, w_got,
    taps, wide, x_own, g_own, mixed, masks, turned, base0, edges0, total0, base1, edges1, total1,
    ready, back, regroup, sliced, part, result,
    load_sem, own_sem, in_send, in_recv, w_send, w_recv,
    m_send, m_recv, t_send, t_recv, o_send, o_recv,
):
    me_c, me_h = lax.axis_index("ctx"), lax.axis_index("head")

    def remote(src, dst, send, recv, axis, k):
        me, n = (me_c, NC) if axis == "ctx" else (me_h, NH)
        return pltpu.make_async_remote_copy(
            src_ref=src, dst_ref=dst, send_sem=send, recv_sem=recv,
            device_id={axis: lax.rem(me + k, n)}, device_id_type=MESH,
        )

    def w_copy(k):
        return remote(w_in, w_got.at[me_h], w_send.at[k], w_recv.at[k], "head", k)

    def in_copy(leg, k):
        rows = pl.ds(*LEGS[leg])
        peer = lax.rem(me_c + k, NC)
        return remote(
            packed.at[peer, rows], got.at[me_c, rows], in_send.at[leg, k], in_recv.at[leg, k], "ctx", k
        )

    def m_copy(t, k):
        rows = pl.ds(pl.multiple_of(t * 2 * ROWS, 16), 2 * ROWS)
        peer = lax.rem(me_c + k, NC)
        return remote(
            ready.at[peer, rows], back.at[me_c, rows], m_send.at[t, k], m_recv.at[t, k], "ctx", k
        )

    def t_copy(k):
        peer = lax.rem(me_h + k, NH)
        return remote(sliced.at[peer], part.at[me_h], t_send.at[k], t_recv.at[k], "head", k)

    columns = pl.ds(pl.multiple_of(me_h * LANES, LANES), LANES)

    def o_copy(k):
        peer = lax.rem(me_h + k, NH)
        return remote(result.at[peer], out.at[:, columns], o_send.at[k], o_recv.at[k], "head", k)

    greet(me_c, me_h)
    loads = [
        pltpu.make_async_copy(a, b, load_sem.at[i])
        for i, (a, b) in enumerate(
            (
                (h_hbm, h_in), (x_hbm, x_in), (far_hbm, far_in), (g_hbm, g_in),
                (skip_hbm, skip_in), (w_hbm, w_in),
            )
        )
    ]
    for copy in loads:
        copy.start()

    def spread(a, ref):
        for s in range(ROWS):
            stage[a, pl.ds(s, CH, stride=ROWS), :] = ref[:, LANES * s : LANES * (s + 1)].astype(F32)

    def pack(a, m):
        lo = TAPS + PER * m + ROWS * a if a < 2 else GATES + ROWS * m
        for c in range(NC):
            ch = MINE * c + m
            packed[c, lo : lo + ROWS, :] = stage[a, ROWS * ch : ROWS * (ch + 1), :].astype(BF16)

    def depart(leg):
        for k in range(1, NC):
            in_copy(leg, k).start()

    loads[2].wait()
    row = lax.broadcasted_iota(jnp.int32, (ROWS, LANES), 0)
    table = jnp.full((ROWS, LANES), -1, jnp.int32)
    for r in range(2):
        for k in range(4):
            table = jnp.where(row == 4 * r + k, far_in[r, k], table)
    table = table.astype(F32).astype(BF16)
    for c in range(NC):
        packed[c, 0:ROWS, :] = table
    for a in range(2):
        loads[a].wait()
        spread(a, (h_in, x_in)[a])
        pack(a, 0)
        pack(a, 1)
    pl.semaphore_wait(pltpu.get_barrier_semaphore(), NC - 1 + NH - 1)
    depart(0)
    for a in range(2):
        for m in range(2, MINE):
            pack(a, m)
    depart(1)
    for copy in loads[3:]:
        copy.wait()
    spread(2, g_in)
    for m in range(MINE):
        pack(2, m)
    depart(2)
    for k in range(1, NH):
        w_copy(k).start()
    own = [
        pltpu.make_async_copy(a, b, own_sem.at[i])
        for i, (a, b) in enumerate(
            (
                (packed.at[me_c], got.at[me_c]), (w_in, w_got.at[me_h]),
            )
        )
    ]
    for copy in own:
        copy.start()
    for copy in own:
        copy.wait()
    empty = jnp.zeros((BLOCKS, LANES), F32)
    for f in range(SUBS):
        for a in range(TILES):
            base0[f, a, 0:BLOCKS, :] = empty
            base1[f, a, 0:BLOCKS, :] = empty
        for b in range(SUBS):
            turned[b, f, 0:BLOCKS, :] = empty
    edges0[0:PART, :] = empty.astype(BF16)
    edges1[0:PART, :] = empty.astype(BF16)

    def arrive(leg):
        for k in range(1, NC):
            in_copy(leg, k).wait()

    arrive(0)
    for c in range(NC):
        regroup[8 * c : 8 * c + 8, :] = got[c, 0:ROWS, :].astype(F32)[0:8]
    read_masks(regroup, masks)

    def read(m, a, to):
        lo = TAPS + m * PER + a * ROWS if a < 2 else GATES + m * ROWS
        rows = pl.ds(pl.multiple_of(lo, 16), ROWS)
        for c in range(NC):
            to[ROWS * c : ROWS * (c + 1), :] = got[c, rows, :].astype(F32)

    def hand_back(m, total):
        finish(m, read, skip_in[MINE * me_c + m], total, x_own, g_own, mixed)
        for c in range(NC):
            ready[c, pl.ds(pl.multiple_of(m * ROWS, 16), ROWS), :] = mixed[
                ROWS * c : ROWS * (c + 1), :
            ].astype(BF16)

    def send_back(t):
        for k in range(1, NC):
            m_copy(t, k).start()

    prepare(0, read, taps, wide, turned, base0, edges0)

    multiply(masks, base0, edges0, total0)
    prepare(1, read, taps, wide, turned, base1, edges1)
    arrive(1)
    arrive(2)
    multiply(masks, base1, edges1, total1)
    prepare(2, read, taps, wide, turned, base0, edges0)
    hand_back(0, total0)
    multiply(masks, base0, edges0, total0)
    prepare(3, read, taps, wide, turned, base1, edges1)
    hand_back(1, total1)
    send_back(0)
    multiply(masks, base1, edges1, total1)
    hand_back(2, total0)
    hand_back(3, total1)
    send_back(1)
    for t in range(2):
        for k in range(1, NC):
            m_copy(t, k).wait()
    for c in range(NC):
        stage[0, 64 * c : 64 * c + 64, :] = jnp.where(
            me_c == c, ready[c].astype(F32), back[c].astype(F32)
        )
    for t in range(NH):
        sliced[t] = stage[0, pl.ds(t, CH, stride=NH), :].astype(BF16)
    for k in range(1, NH):
        t_copy(k).start()
    copy = pltpu.make_async_copy(sliced.at[me_h], part.at[me_h], own_sem.at[3])
    copy.start()
    copy.wait()
    for k in range(1, NH):
        w_copy(k).wait()
    for k in range(1, NH):
        t_copy(k).wait()
    total = lax.dot_general(
        w_got[...].reshape(NH * CH, NH * CH), part[...].reshape(NH * CH, LANES),
        (((0,), (0,)), ((), ())), preferred_element_type=F32,
    )
    for t in range(NH):
        result[t] = total[CH * t : CH * (t + 1), :]
    for k in range(1, NH):
        o_copy(k).start()
    copy = pltpu.make_async_copy(result.at[me_h], out.at[:, columns], own_sem.at[5])
    copy.start()
    copy.wait()
    for k in range(1, NH):
        o_copy(k).wait()


def local(inputs, gate, filter_taps, skip, w_out, far_pairs):
    hbm = pl.BlockSpec(memory_space=pltpu.HBM)
    dma = pltpu.SemaphoreType.DMA
    vmem = pltpu.VMEM
    arrays = (inputs, gate, filter_taps, w_out, far_pairs, skip)
    return pl.pallas_call(
        kernel,
        out_shape=jax.ShapeDtypeStruct((CH, NH * LANES), F32),
        in_specs=[hbm] * 6,
        out_specs=hbm,
        scratch_shapes=[
            vmem(inputs.shape, BF16), vmem(gate.shape, BF16), vmem(filter_taps.shape, F32),
            vmem(w_out.shape, BF16), pltpu.SMEM(far_pairs.shape, jnp.int32), pltpu.SMEM(skip.shape, F32),
            vmem((3, CH * ROWS, LANES), F32),
            vmem((NC, GATES + MINE * ROWS, LANES), BF16),
            vmem((NC, GATES + MINE * ROWS, LANES), BF16),
            vmem((NH, CH, NH * CH), BF16),
            *[vmem((PIECES, LANES), F32)] * 5,
            vmem((TILES, BLOCKS, BLOCKS, LANES), F32),
            vmem((SUBS, SUBS, 2 * BLOCKS, LANES), F32),
            *[
                vmem((SUBS, TILES, 2 * BLOCKS, LANES), F32),
                vmem((PART * (PIECES + 1), LANES), BF16),
                vmem(((SUBS * TILES - 1) * BLOCKS, 2 * LANES), F32),
            ]
            * 2,
            vmem((NC, MINE * ROWS, LANES), BF16),
            vmem((NC, MINE * ROWS, LANES), BF16),
            vmem((NC * 8, LANES), F32),
            vmem((NH, CH, LANES), BF16),
            vmem((NH, CH, LANES), BF16),
            vmem((NH, CH, LANES), F32),
            dma((6,)), dma((6,)), dma((3, NC)), dma((3, NC)), dma((NH,)), dma((NH,)),
            dma((2, NC)), dma((2, NC)), dma((NH,)), dma((NH,)), dma((NH,)), dma((NH,)),
        ],
        compiler_params=pltpu.CompilerParams(
            collective_id=0, has_side_effects=True, vmem_limit_bytes=40 << 20
        ),
    )(*(pltpu.with_memory_space_constraint(a, pltpu.HBM) for a in arrays))


def solution(mesh):
    in_specs = (
        P("head", "ctx"),
        P("head", "ctx"),
        P("head", "ctx"),
        P("head"),
        P("head", None),
        P("ctx", None),
    )
    out_specs = P("head", "ctx")
    return jax.shard_map(local, mesh=mesh, in_specs=in_specs, out_specs=out_specs, check_vma=False)
```
